256 devices in a mesh: seq: 32 (over z_lo, x, core), head: 8 (over y, z_hi).
Axes of the slice: x: 4, y: 4, z: 8 (z_hi: 2, z_lo: 4; z = z_hi * 4 + z_lo), core: 2. Of those that a mesh axis runs over, the one named last changes fastest.
Arguments:
- activations: bfloat16 [16384, 4096], P('seq'), may hold values from -400 to 400
- norm_gain: float32 [4096], replicated, may hold values from 0.1 to 1.9
- shifted: int32 [16], replicated, may hold values from 0 to 1, as said below
- query_weight: bfloat16 [4096, 2048], P('seq', 'head'), may hold values from -0.1875 to 0.1875
- key_weight: bfloat16 [4096, 2048], P('seq', 'head'), may hold values from -0.1875 to 0.1875
- value_weight: bfloat16 [4096, 2048], P('seq', 'head'), may hold values from -0.09375 to 0.09375
- output_weight: bfloat16 [2048, 4096], P('head', 'seq'), may hold values from -0.25 to 0.25
- query_down: bfloat16 [4096, 64], replicated, may hold values from -0.09375 to 0.09375
- query_up: bfloat16 [64, 2048], replicated, may hold values from -0.75 to 0.75
- key_down: bfloat16 [4096, 64], replicated, may hold values from -0.09375 to 0.09375
- key_up: bfloat16 [64, 2048], replicated, may hold values from -0.75 to 0.75
- value_down: bfloat16 [4096, 64], replicated, may hold values from -0.09375 to 0.09375
- value_up: bfloat16 [64, 2048], replicated, may hold values from -0.75 to 0.75
- output_down: bfloat16 [2048, 64], replicated, may hold values from -0.125 to 0.125
- output_up_matrix: bfloat16 [64, 4096], replicated, may hold values from -0.75 to 0.75
Outputs:
- attended: bfloat16 [16384, 4096], P('seq', 'head')
- log_sums: float32 [16384, 16], P('seq', 'head')
The draws below stay inside these ranges and needn't reach their ends.
Inputs may be any that keep to these rules, and one draw needn't show every extreme that they name: Exactly 8 heads are shifted; which ones is drawn.
All inputs are finite; a program needn't handle non-finite values.
Results may differ from the reference program's by a relative error of at most 0.02.
Values may be sent and summed in bfloat16 or wider, within the bound.
A program may use at most 64 MiB of HBM per device.

```python
import math
import jax
import jax.numpy as jnp
from jax import lax

D = 4096
H = 16
HD = 128
R = 64
TOK_DEV = 512
GROUP_DEV = 16
SEQ = 16384
GROUP = 8192
SHIFT = 4096
QW = 2048
N_SEQ = 32
N_HEAD = 8


def draw_activations(key, part):
    key = jax.random.fold_in(key, 3)
    row_key, column_key, main_key = jax.random.split(key, 3)
    row_scale = jnp.exp(jax.random.uniform(row_key, (SEQ, 1), jnp.float32, 0.0, math.log(10.0)))
    column_scale = jnp.exp(jax.random.uniform(column_key, (1, D), jnp.float32, 0.0, math.log(10.0)))
    drawn = jnp.clip(jax.random.normal(main_key, (SEQ, D), jnp.float32), -4.0, 4.0)
    return (drawn * row_scale * column_scale).astype(jnp.bfloat16)


def draw_shifted(key, part):
    key = jax.random.fold_in(key, 5)
    order = jax.random.permutation(key, H)
    return (order < H // 2).astype(jnp.int32)


def draw_query_weight(key, part):
    key = jax.random.fold_in(key, 11)
    drawn = jnp.clip(jax.random.normal(key, (D, QW), jnp.float32), -4.0, 4.0)
    return (drawn * (1.4 / math.sqrt(D))).astype(jnp.bfloat16)


def draw_key_weight(key, part):
    key = jax.random.fold_in(key, 13)
    drawn = jnp.clip(jax.random.normal(key, (D, QW), jnp.float32), -4.0, 4.0)
    return (drawn * (1.4 / math.sqrt(D))).astype(jnp.bfloat16)


def levels(stream_key, extent, pieces, least, largest):
    level = 1.0
    for position, parts in pieces:
        draws = jax.random.uniform(jax.random.fold_in(jax.random.fold_in(stream_key, 6), position), (parts,), jnp.float32, least / len(pieces), largest / len(pieces))
        level = level * jnp.repeat(jnp.exp(draws), extent[position] // parts).reshape((-1,) + (1,) * (len(extent) - 1 - position))
    return level


def scatter_about(key, shape, deviation, most, cuts=(), kind=jnp.bfloat16):
    result = jax.random.normal(key, shape, jnp.float32) * deviation
    if len(cuts) > 0:
        result = levels(key, shape, cuts, -0.22, 0.18) * result
    return jnp.clip(result, min=-most, max=most).astype(kind)


def setup_inputs(seed: int = 0) -> dict:
    streams_of = jax.random.split(jax.random.key(seed), 16)
    activations = draw_activations(jax.random.fold_in(streams_of[15], 71), 0)
    norm_gain = jnp.clip(1.0 + 0.18 * jax.random.normal(streams_of[1], (D,), jnp.float32), 0.1, 1.9)
    shifted = draw_shifted(jax.random.fold_in(streams_of[15], 71), 0)
    query_weight = draw_query_weight(jax.random.fold_in(streams_of[15], 71), 0)
    key_weight = draw_key_weight(jax.random.fold_in(streams_of[15], 71), 0)
    value_weight = scatter_about(streams_of[5], (D, QW), D ** -0.5, 0.09375, ((0, 32), (1, 8)))
    output_weight = scatter_about(streams_of[6], (QW, D), (QW // 4) ** -0.5, 0.25, ((0, 8), (1, 32)))
    query_down = scatter_about(streams_of[7], (D, R), D ** -0.5, 0.09375)
    query_up = scatter_about(streams_of[8], (R, QW), R ** -0.5, 0.75)
    key_down = scatter_about(streams_of[9], (D, R), D ** -0.5, 0.09375)
    key_up = scatter_about(streams_of[10], (R, QW), R ** -0.5, 0.75)
    value_down = scatter_about(streams_of[11], (D, R), D ** -0.5, 0.09375)
    value_up = scatter_about(streams_of[12], (R, QW), R ** -0.5, 0.75)
    output_down = scatter_about(streams_of[13], (QW, R), QW ** -0.5, 0.125)
    output_up_matrix = scatter_about(streams_of[14], (R, D), R ** -0.5, 0.75)
    return dict(activations=activations, norm_gain=norm_gain, shifted=shifted, query_weight=query_weight, key_weight=key_weight, value_weight=value_weight, output_weight=output_weight, query_down=query_down, query_up=query_up, key_down=key_down, key_up=key_up, value_down=value_down, value_up=value_up, output_down=output_down, output_up_matrix=output_up_matrix)


EPS = 1e-05
ADAPTER_SCALING = 0.5
ROPE_BASE = 10000.0
MASKED = -1e+30

def normalize(values, gain):
    widened = values.astype(jnp.float32)
    mean_square = lax.optimization_barrier(jnp.mean(widened * widened, axis=-1, keepdims=True))
    return (widened * lax.rsqrt(mean_square + EPS) * gain).astype(jnp.bfloat16)

def adapted(normed, weight, down_factor, up_projection_factor):
    direct_path = jnp.dot(normed, weight, preferred_element_type=jnp.float32)
    reduced_result = jnp.dot(normed, down_factor, preferred_element_type=jnp.float32).astype(jnp.bfloat16)
    return direct_path + ADAPTER_SCALING * jnp.dot(reduced_result, up_projection_factor, preferred_element_type=jnp.float32)

def rotate(values, positions, head_size):
    halfway = head_size // 2
    frequency = ROPE_BASE ** (-2.0 * jnp.arange(halfway).astype(jnp.float32) / head_size)
    angles = positions.astype(jnp.float32)[:, None] * frequency[None, :]
    cosine = jnp.cos(angles)[:, None, :]
    sine = jnp.sin(angles)[:, None, :]
    shaped = values.reshape(values.shape[0], -1, head_size)
    leading = shaped[..., :halfway]
    trailing = shaped[..., halfway:]
    turned = jnp.concatenate([leading * cosine - trailing * sine, trailing * cosine + leading * sine], axis=-1)
    return turned.reshape(values.shape).astype(jnp.bfloat16)

def attend_head(operands):
    query_head, key_head, value_head, flag = operands
    doubled_keys = jnp.concatenate([key_head, key_head], axis=0)
    doubled_values = jnp.concatenate([value_head, value_head], axis=0)
    offset = flag * SHIFT
    scale = 1.0 / math.sqrt(HD)

    def one_slab(slab):
        query_rows = lax.dynamic_slice_in_dim(query_head, slab * TOK_DEV, TOK_DEV, 0)
        window_start = (slab - GROUP_DEV + 1 + N_SEQ) % N_SEQ * TOK_DEV
        key_rows = lax.dynamic_slice_in_dim(doubled_keys, window_start, GROUP, 0)
        value_rows = lax.dynamic_slice_in_dim(doubled_values, window_start, GROUP, 0)
        query_pos = slab * TOK_DEV + jnp.arange(TOK_DEV, dtype=jnp.int32)
        key_pos = (window_start + jnp.arange(GROUP, dtype=jnp.int32)) % SEQ
        query_rel = (query_pos - offset + SEQ) % SEQ
        key_rel = (key_pos - offset + SEQ) % SEQ
        allowed = (query_rel[:, None] // GROUP == key_rel[None, :] // GROUP) & (key_rel[None, :] <= query_rel[:, None])
        scores = jnp.dot(query_rows, key_rows.T, preferred_element_type=jnp.float32) * scale
        scores = jnp.where(allowed, scores, MASKED)
        highest = lax.optimization_barrier(jnp.max(scores, axis=1, keepdims=True))
        weights = jnp.where(allowed, jnp.exp(scores - highest), 0.0)
        row_total = lax.optimization_barrier(jnp.sum(weights, axis=1, keepdims=True))
        mixed = jnp.dot(weights.astype(jnp.bfloat16), value_rows, preferred_element_type=jnp.float32) / row_total
        return (mixed.astype(jnp.bfloat16), highest[:, 0] + jnp.log(row_total[:, 0]))
    mixed_slabs, sums_slabs = lax.map(one_slab, jnp.arange(N_SEQ, dtype=jnp.int32))
    return (mixed_slabs.reshape(SEQ, HD), sums_slabs.reshape(SEQ))

def reference(activations, norm_gain, shifted, query_weight, key_weight, value_weight, output_weight, query_down, query_up, key_down, key_up, value_down, value_up, output_down, output_up_matrix):
    normed = normalize(activations, norm_gain)
    positions = jnp.arange(SEQ, dtype=jnp.int32)
    queries = rotate(adapted(normed, query_weight, query_down, query_up), positions, HD)
    keys_all = rotate(adapted(normed, key_weight, key_down, key_up), positions, HD)
    values_all = adapted(normed, value_weight, value_down, value_up).astype(jnp.bfloat16)
    query_heads = queries.reshape(SEQ, H, HD).transpose(1, 0, 2)
    key_heads = keys_all.reshape(SEQ, H, HD).transpose(1, 0, 2)
    value_heads = values_all.reshape(SEQ, H, HD).transpose(1, 0, 2)
    mixed_heads, head_sums = lax.map(attend_head, (query_heads, key_heads, value_heads, shifted))
    mixed = mixed_heads.transpose(1, 0, 2).reshape(SEQ, H * HD)
    group_width = H * HD // N_HEAD
    summed = jnp.zeros((SEQ, D), jnp.float32)
    for group_index in range(N_HEAD):
        lower = group_index * group_width
        mixed_part = mixed[:, lower:lower + group_width]
        reduced_result = jnp.dot(mixed_part, output_down[lower:lower + group_width], preferred_element_type=jnp.float32).astype(jnp.bfloat16)
        partial_total_sum = jnp.dot(mixed_part, output_weight[lower:lower + group_width], preferred_element_type=jnp.float32)
        partial_total_sum = partial_total_sum + ADAPTER_SCALING * jnp.dot(reduced_result, output_up_matrix, preferred_element_type=jnp.float32)
        rounded = lax.optimization_barrier(partial_total_sum.astype(jnp.bfloat16))
        summed = summed + rounded.astype(jnp.float32)
    return (summed.astype(jnp.bfloat16), head_sums.T)
```

```python
import math

import jax
import jax.numpy as jnp
import numpy as np
from jax import lax
from jax.experimental import pallas as pl
from jax.experimental.pallas import tpu as pltpu
from jax.sharding import PartitionSpec as P

EPS = 1e-05
ADAPTER_SCALING = 0.5
ROPE_BASE = 10000.0
MASKED = -1e30
D = 4096
HD = 128
TOK = 512
CHIP = 2 * TOK
MESH = pl.DeviceIdType.MESH
F32 = jnp.float32
BF16 = jnp.bfloat16
VMEM_BYTES = 56 * 1024 * 1024


def spot():
    seq = lax.axis_index("seq")
    head = lax.axis_index("head")
    return seq // 8, (seq // 2) % 4, seq % 2, head // 2, head % 2


def seq_of(z, x, core):
    return z * 8 + x * 2 + core


def greet(partners):
    barrier = pltpu.get_barrier_semaphore()
    for partner in partners:
        pl.semaphore_signal(barrier, inc=1, device_id=partner, device_id_type=MESH)
    pl.semaphore_wait(barrier, len(partners))


def remote(source, target, send, receive, device):
    return pltpu.make_async_remote_copy(
        src_ref=source,
        dst_ref=target,
        send_sem=send,
        recv_sem=receive,
        device_id=device,
        device_id_type=MESH,
    )


def dot(a, b):
    return jnp.dot(a, b, preferred_element_type=F32)


def dot_nt(a, b):
    return lax.dot_general(a, b, (((1,), (1,)), ((), ())), preferred_element_type=F32)


def times(value, n):
    return jnp.concatenate([value] * n, axis=1)


class Ring:
    def __init__(self, view, receive, send, place, right, left):
        self.view, self.receive, self.send = view, receive, send
        self.place, self.right, self.left = place, right, left
        self.open = []

    def slot(self, d, step):
        return d * 4 + (self.place + step) % 4

    def start(self, source, target, receive, device):
        copy = remote(source, target, self.send.at[len(self.open)], receive, device)
        copy.start()
        self.open.append(copy)

    def push(self, d, step, device):
        slot = self.slot(d, step)
        self.start(self.view(slot), self.view(slot), self.receive.at[slot], device)

    def push_own(self, d):
        self.push(d, 0, self.right)
        self.push(d, 0, self.left)

    def arrived(self, d, step):
        slot = self.slot(d, step)
        ref = self.view(slot)
        remote(ref, ref, self.send.at[0], self.receive.at[slot], self.right).wait_recv()

    def own(self, d):
        self.arrived(d, 0)
        self.push_own(d)

    def from_left(self, d):
        self.arrived(d, 3)
        if d % 2 == 0:
            self.push(d, 3, self.right)

    def from_right(self, d):
        self.arrived(d, 1)
        if d % 2 == 1:
            self.push(d, 1, self.left)

    def across(self, d):
        self.arrived(d, 2)

    def finish(self):
        for copy in self.open:
            copy.wait_send()


def project_kernel(
    act, gain, wq, wk, wv, down_q, down_k, down_v, up_q, up_k, up_v, tables, bases,
    q_out, k_out, v_out,
    raw, normed, stage, weights, downs, down_all, up_all, total,
    load, receive, send, norm_receive, norm_send,
):
    z, x, core, y, zh = spot()
    head = lax.axis_index("head")
    sibling = (seq_of(z, x, 1 - core), head)
    right = (seq_of(z, (x + 1) % 4, core), head)
    left = (seq_of(z, (x + 3) % 4, core), head)

    loads = []
    for part in range(4):
        rows = pl.ds(part * 128, 128)
        loads.append(pltpu.make_async_copy(act.at[rows], raw.at[rows], load.at[part]))
    for index, ref in enumerate((down_q, down_k, down_v)):
        loads.append(pltpu.make_async_copy(ref, downs.at[index], load.at[4 + index]))
    up_all[...] = jnp.zeros_like(up_all)
    columns = pl.ds(pl.multiple_of(head * 256 + core * 128, 128), 128)
    for index, ref in enumerate((up_q, up_k, up_v)):
        target = up_all.at[pl.ds(index * 64, 64), pl.ds(index * 128, 128)]
        loads.append(pltpu.make_async_copy(ref.at[:, columns], target, load.at[7 + index]))
    for copy in loads:
        copy.start()
    for side in range(2):
        for index, ref in enumerate((wq, wk, wv)):
            stage[side, :, index * 128 : index * 128 + 128] = ref[:, side * 128 : side * 128 + 128]

    planes = [(z + e) % 4 for e in range(1, 4)]
    greet(
        [sibling, right, left]
        + [(seq_of(plane, x, side), head) for plane in planes for side in range(2)]
    )

    ring = Ring(lambda slot: weights.at[slot], receive, send, x, right, left)
    half = pl.ds(pl.multiple_of(core * 128, 128), 128)
    other = pl.ds(pl.multiple_of(128 - core * 128, 128), 128)
    ring.start(stage.at[1 - core], weights.at[x, half], receive.at[x], sibling)
    for e, plane in zip(range(1, 4), planes):
        for side in range(2):
            slot = e * 4 + x
            ring.start(
                stage.at[side],
                weights.at[slot, half],
                receive.at[slot],
                (seq_of(plane, x, side), head),
            )
    weights[x, half, :] = stage[core]

    norm_copies = []

    def normalize(part):
        loads[part].wait()

        def tile(index, carry):
            row = part * 128 + index * 16
            wide = raw[pl.ds(row, 16), :].astype(F32)
            mean_square = jnp.mean(wide * wide, axis=-1, keepdims=True)
            result = (wide * lax.rsqrt(mean_square + EPS) * gain[...]).astype(BF16)
            place = pl.ds(pl.multiple_of(core * TOK + row, 16), 16)
            for chunk in range(16):
                normed[chunk, place, :] = result[:, chunk * 256 : chunk * 256 + 256]
            return carry

        lax.fori_loop(0, 8, tile, 0)
        rows = pl.ds(pl.multiple_of(core * TOK + part * 128, 128), 128)
        copy = remote(
            normed.at[:, rows],
            normed.at[:, rows],
            norm_send.at[part],
            norm_receive.at[part],
            sibling,
        )
        copy.start()
        norm_copies.append(copy)

    def reduced(side):
        for block in range(2):
            rows = pl.ds(pl.multiple_of(side * TOK + block * 256, 256), 256)

            def step(chunk, carry):
                return carry + dot(normed[chunk, rows, :], down_all[chunk])

            low = lax.fori_loop(0, 16, step, jnp.zeros((256, 192), F32)).astype(BF16)
            total[rows, :] = ADAPTER_SCALING * dot(low, up_all[...])

    def accumulate(d):
        def block(index, carry):
            rows = pl.ds(pl.multiple_of(index * 256, 256), 256)
            value = total[rows, :]
            for step in range(4):
                slot = ring.slot(d, step)
                chunk = ((z + 4 - d) % 4) * 4 + (x + step) % 4
                value = value + dot(normed[chunk, rows, :], weights[slot])
            total[rows, :] = value
            return carry

        lax.fori_loop(0, 4, block, 0)

    normalize(0)
    piece = weights.at[x, other]
    remote(piece, piece, send.at[0], receive.at[x], sibling).wait_recv()
    ring.push_own(0)
    normalize(1)
    normalize(2)
    ring.own(1)
    normalize(3)
    ring.from_left(0)
    ring.from_right(0)
    for copy in loads[4:]:
        copy.wait()

    def join(chunk, carry):
        rows = pl.ds(pl.multiple_of(chunk * 256, 256), 256)
        down_all[chunk] = jnp.concatenate([downs[index, rows, :] for index in range(3)], axis=1)
        return carry

    lax.fori_loop(0, 16, join, 0)
    reduced(core)
    ring.own(2)
    for part in range(4):
        rows = pl.ds(pl.multiple_of((1 - core) * TOK + part * 128, 128), 128)
        ref = normed.at[:, rows]
        remote(ref, ref, norm_send.at[part], norm_receive.at[part], sibling).wait_recv()
    reduced(1 - core)
    ring.from_left(1)
    ring.from_right(1)
    ring.own(3)
    ring.across(0)
    accumulate(0)
    ring.from_left(2)
    ring.from_right(2)
    ring.across(1)
    accumulate(1)
    ring.from_left(3)
    ring.from_right(3)
    ring.across(2)
    accumulate(2)
    ring.across(3)
    accumulate(3)

    base = bases[pl.ds(z * 4 + x, 1)]
    base_cos, base_sin = base[0, 0:1, :], base[0, 1:2, :]

    def turn(index, carry):
        rows = pl.ds(pl.multiple_of(index * 128, 128), 128)
        cos_row, sin_row = tables[0, rows, :], tables[1, rows, :]
        cos = cos_row * base_cos - sin_row * base_sin
        sin = sin_row * base_cos + cos_row * base_sin
        for number, ref in enumerate((q_out, k_out)):
            value = total[rows, number * 128 : number * 128 + 128]
            value = value * cos + pltpu.roll(value, 64, 1) * sin
            if number == 0:
                value = value * (math.log2(math.e) / math.sqrt(HD))
            ref[rows, :] = value.astype(BF16)
        v_out[rows, :] = total[rows, 256:384].astype(BF16)
        return carry

    lax.fori_loop(0, 8, turn, 0)
    ring.finish()
    for copy in norm_copies:
        copy.wait_send()


def attend_kernel(
    shifted, q, k, v, mixed, log_sums, kv, top, total, load, receive, send
):
    z, x, core, y, zh = spot()
    head = lax.axis_index("head")
    right = (seq_of(z, (x + 1) % 4, core), head)
    left = (seq_of(z, (x + 3) % 4, core), head)
    after = (seq_of((z + 1) % 4, x, core), head)
    before = (seq_of((z + 3) % 4, x, core), head)

    loads = []
    for part in range(2):
        rows = pl.ds(part * TOK, TOK)
        slot = part * 4 + x
        for index, ref in enumerate((k, v)):
            target = kv.at[slot, :, pl.ds(index * 128, 128)]
            loads.append(pltpu.make_async_copy(ref.at[rows], target, load.at[part * 2 + index]))
    for copy in loads:
        copy.start()

    def ones(slot, carry):
        kv[slot, :, 256:384] = jnp.ones((TOK, 128), BF16)
        return carry

    lax.fori_loop(0, 16, ones, 0)
    greet([right, left, after, before])
    for copy in loads:
        copy.wait()

    ring = Ring(lambda slot: kv.at[slot, :, pl.ds(0, 256)], receive, send, x, right, left)
    for part in range(2):
        source, slot = ring.view(ring.slot(part, 0)), ring.slot(part + 2, 0)
        ring.push_own(part)
        ring.start(source, ring.view(slot), receive.at[slot], after)

    for index in range(4):
        rows = pl.ds(index * 256, 256)
        keys = index * 256 + 256
        pieces = []
        for part in range((keys + TOK - 1) // TOK):
            count = min(keys - part * TOK, TOK)
            slot = ring.slot(part, 0)
            scores = dot_nt(q[rows, :], kv[slot, 0:count, 0:128])
            row = index * 256 + lax.broadcasted_iota(jnp.int32, scores.shape, 0)
            column = part * TOK + lax.broadcasted_iota(jnp.int32, scores.shape, 1)
            pieces.append((slot, count, jnp.where(column <= row, scores, MASKED)))
        highest = jnp.max(pieces[0][2], axis=1, keepdims=True)
        for slot, count, scores in pieces[1:]:
            highest = jnp.maximum(highest, jnp.max(scores, axis=1, keepdims=True))
        highest = jnp.broadcast_to(highest, (256, 128))
        value = jnp.zeros((256, 256), F32)
        for slot, count, scores in pieces:
            soft = jnp.exp2(scores - times(highest, count // 128)).astype(BF16)
            value = value + dot(soft, kv[slot, 0:count, 128:384])
        top[rows, :] = highest
        total[rows, :] = value

    def attend(d, step, bias):
        first, second = ring.slot(d, step), ring.slot(d + 1, step)

        def block(index, carry):
            rows = pl.ds(pl.multiple_of(index * 256, 256), 256)
            query = q[rows, :]
            one = dot_nt(query, kv[first, :, 0:128])
            two = dot_nt(query, kv[second, :, 0:128])
            highest = jnp.max(jnp.maximum(one, two), axis=1, keepdims=True)
            old = top[rows, :]
            new = jnp.maximum(old, highest + bias)
            level = times(new - bias, 4)
            value = total[rows, :] * times(jnp.exp2(old - new), 2)
            value = value + dot(jnp.exp2(one - level).astype(BF16), kv[first, :, 128:384])
            value = value + dot(jnp.exp2(two - level).astype(BF16), kv[second, :, 128:384])
            top[rows, :] = new
            total[rows, :] = value
            return carry

        lax.fori_loop(0, 4, block, 0)

    def attend_own_plane(step):
        @pl.when((x + step) % 4 < x)
        def _():
            attend(0, step, 0.0)

    flag = shifted[head * 2 + core]
    reaches = (z % 2) * (1 - flag) + (1 - z % 2) * flag
    bias = (reaches.astype(F32) - 1.0) * (-MASKED)

    ring.from_left(0)
    ring.from_right(1)
    ring.from_left(1)
    ring.from_right(0)
    ring.own(2)
    ring.own(3)
    attend_own_plane(3)
    attend_own_plane(1)
    attend(2, 0, bias)
    ring.across(0)
    ring.across(1)
    ring.from_left(2)
    ring.from_right(3)
    attend_own_plane(2)
    ring.from_left(3)
    attend(2, 3, bias)
    ring.from_right(2)
    attend(2, 1, bias)
    ring.across(2)
    ring.across(3)
    attend(2, 2, bias)

    def close(index, carry):
        rows = pl.ds(pl.multiple_of(index * 256, 256), 256)
        weight = total[rows, 128:256]
        mixed[rows, :] = (total[rows, 0:128] / weight).astype(BF16)
        log_sums[rows, :] = (top[rows, :] + jnp.log2(weight)) * math.log(2.0)
        return carry

    lax.fori_loop(0, 4, close, 0)
    ring.finish()


def output_kernel(
    mixed, log_sums, weight, down, up, out, sums_out, held, sums, up_here, low, total,
    load, receive, send, sums_receive,
):
    z, x, core, y, zh = spot()
    seq = lax.axis_index("seq")
    head = lax.axis_index("head")
    sibling = (seq_of(z, x, 1 - core), head)
    right = (seq, ((y + 1) % 4) * 2 + zh)
    left = (seq, ((y + 3) % 4) * 2 + zh)
    partners = [(seq_of(z, x, side), y * 2 + 1 - zh) for side in range(2)]
    greet([sibling, right, left] + partners)

    ring = Ring(lambda slot: held.at[slot], receive, send, y, right, left)
    columns = pl.ds(pl.multiple_of(core * 128, 128), 128)
    others = pl.ds(pl.multiple_of(128 - core * 128, 128), 128)
    loads = []
    for part in range(2):
        slot = ring.slot(2 + part, 0)
        for side in range(2):
            source = mixed.at[pl.ds(side * TOK + part * 256, 256)]
            ring.start(source, held.at[slot, :, columns], receive.at[slot], partners[side])
    for part in range(2):
        slot = ring.slot(part, 0)
        source = mixed.at[pl.ds(pl.multiple_of((1 - core) * TOK + part * 256, 256), 256)]
        ring.start(source, held.at[slot, :, columns], receive.at[slot], sibling)
        source = mixed.at[pl.ds(pl.multiple_of(core * TOK + part * 256, 256), 256)]
        loads.append(pltpu.make_async_copy(source, held.at[slot, :, columns], load.at[part]))
    source = log_sums.at[pl.ds(pl.multiple_of((1 - core) * TOK, TOK), TOK)]
    ring.start(source, sums.at[core], sums_receive, sibling)
    source = log_sums.at[pl.ds(pl.multiple_of(core * TOK, TOK), TOK)]
    loads.append(pltpu.make_async_copy(source, sums.at[core], load.at[2]))
    source = up.at[:, pl.ds(pl.multiple_of(head * 512, 512), 512)]
    loads.append(pltpu.make_async_copy(source, up_here, load.at[3]))
    for copy in loads:
        copy.start()
    total[...] = jnp.zeros_like(total)
    low[...] = jnp.zeros_like(low)
    for copy in loads:
        copy.wait()
    for part in range(2):
        slot = ring.slot(part, 0)
        piece = held.at[slot, :, others]
        remote(piece, piece, send.at[0], receive.at[slot], sibling).wait_recv()
        ring.push_own(part)

    def add(d, step):
        rows = pl.ds((d % 2) * 256, 256)
        group = ((y + step) % 4) * 2 + (zh + d // 2) % 2
        block = held[ring.slot(d, step)]
        matrix = jnp.concatenate([weight[group * 4 + j] for j in range(4)], axis=1)
        total[rows, :] += dot(block, matrix)
        low[rows, :] += dot(block, down[group])

    ring.own(2)
    ring.own(3)
    add(0, 0)
    add(1, 0)
    for d in range(2):
        ring.from_left(d)
        ring.from_right(d)
        add(d, 3)
        add(d, 1)
    add(2, 0)
    add(3, 0)
    for d in range(2):
        ring.across(d)
        add(d, 2)
    for d in range(2, 4):
        ring.from_left(d)
        ring.from_right(d)
        add(d, 3)
        add(d, 1)
    for d in range(2, 4):
        ring.across(d)
        add(d, 2)

    remote(sums.at[1 - core], sums.at[1 - core], send.at[0], sums_receive, sibling).wait_recv()
    lane = lax.broadcasted_iota(jnp.int32, (TOK, 128), 1)
    sums_out[...] = jnp.where(lane == 0, sums[0], sums[1])[:, 0:2]
    out[...] = (
        total[...] + ADAPTER_SCALING * dot(low[...].astype(BF16), up_here[...])
    ).astype(BF16)
    ring.finish()


def rope_tables():
    frequency = ROPE_BASE ** (-2.0 * np.arange(64, dtype=np.float64) / HD)
    sign = np.concatenate([-np.ones(64), np.ones(64)])

    def table(positions):
        angles = positions[:, None] * np.concatenate([frequency, frequency])[None, :]
        return np.cos(angles), np.sin(angles) * sign

    tables = np.stack(table(np.arange(CHIP, dtype=np.float64)))
    bases = np.stack(table(np.arange(16, dtype=np.float64) * CHIP), axis=1)
    return tables.astype(np.float32), bases.astype(np.float32)


VMEM = pl.BlockSpec(memory_space=pltpu.VMEM)
ANY = pl.BlockSpec(memory_space=pl.ANY)
SMEM = pl.BlockSpec(memory_space=pltpu.SMEM)
DMA = pltpu.SemaphoreType.DMA


def call(kernel, outs, in_specs, scratch, number):
    return pl.pallas_call(
        kernel,
        out_shape=tuple(jax.ShapeDtypeStruct(shape, kind) for shape, kind in outs),
        in_specs=in_specs,
        out_specs=tuple(VMEM for _ in outs),
        scratch_shapes=scratch,
        compiler_params=pltpu.CompilerParams(
            collective_id=number, has_side_effects=True, vmem_limit_bytes=VMEM_BYTES
        ),
    )


def body(
    activations,
    norm_gain,
    shifted,
    query_weight,
    key_weight,
    value_weight,
    output_weight,
    query_down,
    query_up,
    key_down,
    key_up,
    value_down,
    value_up,
    output_down,
    output_up_matrix,
):
    pairs = []
    for h in range(8):
        for j in range(4):
            for g in range(8):
                pairs.append(((h * 4 + j) * 8 + g, (g * 4 + j) * 8 + h))
    turned = lax.ppermute(output_weight, ("seq", "head"), pairs)
    columns = lax.all_gather(turned, "seq", axis=0)

    tables, bases = rope_tables()
    half = ((CHIP, HD), BF16)
    q, k, v = call(
        project_kernel,
        [half, half, half],
        [ANY] + [VMEM] * 4 + [ANY] * 6 + [VMEM] * 2,
        [
            pltpu.VMEM((TOK, D), BF16),
            pltpu.VMEM((16, CHIP, 256), BF16),
            pltpu.VMEM((2, 128, 384), BF16),
            pltpu.VMEM((16, 256, 384), BF16),
            pltpu.VMEM((3, D, 64), BF16),
            pltpu.VMEM((16, 256, 192), BF16),
            pltpu.VMEM((192, 384), BF16),
            pltpu.VMEM((CHIP, 384), F32),
            DMA((10,)),
            DMA((16,)),
            DMA((20,)),
            DMA((4,)),
            DMA((4,)),
        ],
        1,
    )(
        activations,
        norm_gain.reshape(1, D),
        query_weight,
        key_weight,
        value_weight,
        query_down,
        key_down,
        value_down,
        query_up,
        key_up,
        value_up,
        jnp.asarray(tables),
        jnp.asarray(bases),
    )
    mixed, log_sums = call(
        attend_kernel,
        [half, ((CHIP, 128), F32)],
        [SMEM, VMEM, ANY, ANY],
        [
            pltpu.VMEM((16, TOK, 384), BF16),
            pltpu.VMEM((CHIP, 128), F32),
            pltpu.VMEM((CHIP, 256), F32),
            DMA((4,)),
            DMA((16,)),
            DMA((20,)),
        ],
        2,
    )(shifted, q, k, v)
    return call(
        output_kernel,
        [((TOK, 512), BF16), ((TOK, 2), F32)],
        [ANY, ANY, VMEM, VMEM, ANY],
        [
            pltpu.VMEM((16, 256, 256), BF16),
            pltpu.VMEM((2, TOK, 128), F32),
            pltpu.VMEM((64, 512), BF16),
            pltpu.VMEM((TOK, 64), F32),
            pltpu.VMEM((TOK, 512), F32),
            DMA((4,)),
            DMA((16,)),
            DMA((20,)),
            DMA,
        ],
        3,
    )(mixed, log_sums, columns, output_down.reshape(8, 256, 64), output_up_matrix)


def solution(mesh):
    placed = (
        P("seq", None),
        P(),
        P(),
        P("seq", "head"),
        P("seq", "head"),
        P("seq", "head"),
        P("head", "seq"),
        P(),
        P(),
        P(),
        P(),
        P(),
        P(),
        P(),
        P(),
    )
    return jax.shard_map(
        body,
        mesh=mesh,
        in_specs=placed,
        out_specs=(P("seq", "head"), P("seq", "head")),
        check_vma=False,
    )
```

```python
import math

import jax
import jax.numpy as jnp
import numpy as np
from jax import lax
from jax.experimental import pallas as pl
from jax.experimental.pallas import tpu as pltpu
from jax.sharding import PartitionSpec as P

EPS = 1e-05
ADAPTER_SCALING = 0.5
ROPE_BASE = 10000.0
MASKED = -1e30
D = 4096
HD = 128
TOK = 512
MESH = pl.DeviceIdType.MESH
F32 = jnp.float32
BF16 = jnp.bfloat16
VMEM_BYTES = 56 * 1024 * 1024


def spot():
    seq = lax.axis_index("seq")
    head = lax.axis_index("head")
    return seq // 8, (seq // 2) % 4, seq % 2, head // 2, head % 2


def seq_of(z, x, core):
    return z * 8 + x * 2 + core


def remote(source, target, send, receive, device):
    return pltpu.make_async_remote_copy(
        src_ref=source,
        dst_ref=target,
        send_sem=send,
        recv_sem=receive,
        device_id=device,
        device_id_type=MESH,
    )


def dot(a, b):
    return jnp.dot(a, b, preferred_element_type=F32)


def dot_nt(a, b):
    return lax.dot_general(a, b, (((1,), (1,)), ((), ())), preferred_element_type=F32)


def times(value, n):
    return jnp.concatenate([value] * n, axis=1)


class Ring:
    def __init__(self, views, receive, send, place, right, left, twin=None, sibling=None):
        self.view, self.other = views
        self.receive, self.send = receive, send
        self.place, self.right, self.left = place, right, left
        self.twin, self.sibling = twin, sibling
        self.open = []

    def slot(self, d, step):
        return d * 4 + (self.place + step) % 4

    def start(self, source, target, receive, device):
        copy = remote(source, target, self.send(len(self.open)), receive, device)
        copy.start()
        self.open.append(copy)

    def push(self, d, step, device):
        slot = self.slot(d, step)
        self.start(self.view(slot), self.view(slot), self.receive(slot), device)

    def push_far(self, d, step, far, device):
        slot, there = self.slot(d, step), self.slot(far, step)
        self.start(self.view(slot), self.view(there), self.receive(there), device)

    def push_own(self, d):
        self.push(d, 0, self.right)
        self.push(d, 0, self.left)

    def hand(self, d, step):
        if self.sibling is not None:
            slot = self.slot(d, step)
            self.start(self.view(slot), self.view(slot), self.twin(slot), self.sibling)

    def handed(self, d, step):
        slot = self.slot(d, step)
        ref = self.other(slot)
        remote(ref, ref, self.send(0), self.twin(slot), self.sibling).wait_recv()

    def arrived(self, d, step):
        slot = self.slot(d, step)
        ref = self.view(slot)
        remote(ref, ref, self.send(0), self.receive(slot), self.right).wait_recv()

    def own(self, d):
        self.arrived(d, 0)
        self.push_own(d)
        self.hand(d, 0)

    def from_left(self, d, forward=True):
        self.arrived(d, 3)
        if forward and d % 2 == 0:
            self.push(d, 3, self.right)
        self.hand(d, 3)

    def from_right(self, d, forward=True):
        self.arrived(d, 1)
        if forward and d % 2 == 1:
            self.push(d, 1, self.left)
        self.hand(d, 1)

    def across(self, d):
        self.arrived(d, 2)
        self.hand(d, 2)

    def finish(self):
        for copy in self.open:
            copy.wait_send()


INPUTS = [
    "act",
    "gain",
    "shifted",
    "wq",
    "wk",
    "wv",
    "wo",
    "down_q",
    "up_q",
    "down_k",
    "up_k",
    "down_v",
    "up_v",
    "down_o",
    "up_o",
    "tables",
    "bases",
]
OUTPUTS = ["out", "sums_out"]
DMA = pltpu.SemaphoreType.DMA
SCRATCH = dict(
    raw=pltpu.VMEM((TOK, D), BF16),
    normed=pltpu.VMEM((16, TOK, 256), BF16),
    weights=pltpu.VMEM((2, 16, 256, 384), BF16),
    down_all=pltpu.VMEM((192, D), BF16),
    up_all=pltpu.VMEM((2, 192, 384), BF16),
    total=pltpu.VMEM((2, TOK, 384), F32),
    q=pltpu.VMEM((2, TOK, HD), BF16),
    kv=pltpu.VMEM((2, 2, 16, 256, 384), BF16),
    top=pltpu.VMEM((TOK, 128), F32),
    mix=pltpu.VMEM((TOK, 256), F32),
    columns=pltpu.VMEM((32, 256, 128), BF16),
    held=pltpu.VMEM((2, 16, 256, 128), BF16),
    up_here=pltpu.VMEM((64, 512), BF16),
    low=pltpu.VMEM((TOK, 64), F32),
    result=pltpu.VMEM((TOK, 512), F32),
    load=DMA((15,)),
    weight_receive=DMA((2, 16)),
    weight_twin=DMA((2, 16)),
    weight_send=DMA((2, 31)),
    key_receive=DMA((2, 16)),
    key_twin=DMA((2, 16)),
    key_send=DMA((2, 30)),
    mix_receive=DMA((2, 16)),
    mix_send=DMA((2, 14)),
    column_receive=DMA((16,)),
    column_twin=DMA((16,)),
    column_send=DMA((32,)),
)


class Refs:
    pass


def kernel(*refs):
    r = Refs()
    for name, ref in zip(INPUTS + OUTPUTS + list(SCRATCH), refs):
        setattr(r, name, ref)
    z, x, core, y, zh = spot()
    seq = lax.axis_index("seq")
    head = lax.axis_index("head")
    sibling = (seq_of(z, x, 1 - core), head)
    right = (seq_of(z, (x + 1) % 4, core), head)
    left = (seq_of(z, (x + 3) % 4, core), head)
    planes = [(seq_of((z + e) % 4, x, core), head) for e in range(1, 4)]
    up_y = (seq, ((y + 1) % 4) * 2 + zh)
    down_y = (seq, ((y + 3) % 4) * 2 + zh)
    partner = (seq, y * 2 + 1 - zh)
    turn_seq = head * 4 + seq % 4
    turned = (turn_seq, seq // 4)
    stays = seq // 4 == head

    loads = []
    for part in range(4):
        rows = pl.ds(part * 128, 128)
        loads.append(pltpu.make_async_copy(r.act.at[rows], r.raw.at[rows], r.load.at[part]))
    for index, ref in enumerate((r.down_k, r.down_v, r.down_q)):
        target = r.down_all.at[pl.ds(index * 64, 64)]
        loads.append(pltpu.make_async_copy(ref, target, r.load.at[4 + index]))
    r.up_all[...] = jnp.zeros_like(r.up_all)
    for side in range(2):
        here = pl.ds(pl.multiple_of(head * 256 + side * 128, 128), 128)
        for index, ref in enumerate((r.up_k, r.up_v, r.up_q)):
            target = r.up_all.at[side, pl.ds(index * 64, 64), pl.ds(index * 128, 128)]
            loads.append(
                pltpu.make_async_copy(
                    ref.at[:, here], target, r.load.at[7 + side * 3 + index]
                )
            )
    source = r.up_o.at[:, pl.ds(pl.multiple_of(head * 512, 512), 512)]
    loads.append(pltpu.make_async_copy(source, r.up_here, r.load.at[13]))
    for copy in loads:
        copy.start()
    own_rows = pl.ds(pl.multiple_of(core * 128, 128), 128)
    other_rows = pl.ds(pl.multiple_of(128 - core * 128, 128), 128)
    for side in range(2):
        for index, ref in enumerate((r.wk, r.wv, r.wq)):
            r.weights[side, x, own_rows, index * 128 : index * 128 + 128] = ref[
                :, side * 128 : side * 128 + 128
            ]

    def ones(slot, carry):
        for side in range(2):
            for which in range(2):
                r.kv[side, which, slot, :, 256:384] = jnp.ones((256, 128), BF16)
        return carry

    lax.fori_loop(0, 16, ones, 0)

    barrier = pltpu.get_barrier_semaphore()
    everyone = [sibling, right, left, up_y, down_y, partner] + planes
    for device in everyone:
        pl.semaphore_signal(barrier, inc=1, device_id=device, device_id_type=MESH)

    @pl.when(jnp.logical_not(stays))
    def _():
        pl.semaphore_signal(barrier, inc=1, device_id=turned, device_id_type=MESH)

    pl.semaphore_wait(barrier, len(everyone) + 1 - stays.astype(jnp.int32))

    def weight_ring(side):
        return Ring(
            (
                lambda slot: r.weights.at[side, slot, own_rows],
                lambda slot: r.weights.at[side, slot, other_rows],
            ),
            lambda slot: r.weight_receive.at[side, slot],
            lambda index: r.weight_send.at[side, index],
            x, right, left,
            lambda slot: r.weight_twin.at[side, slot],
            sibling,
        )

    def key_ring(side):
        return Ring(
            (
                lambda slot: r.kv.at[side, core, slot, :, pl.ds(0, 256)],
                lambda slot: r.kv.at[side, 1 - core, slot, :, pl.ds(0, 256)],
            ),
            lambda slot: r.key_receive.at[side, slot],
            lambda index: r.key_send.at[side, index],
            x, right, left,
            lambda slot: r.key_twin.at[side, slot],
            sibling,
        )

    def mix_ring(side):
        return Ring(
            (lambda slot: r.held.at[side, slot], None),
            lambda slot: r.mix_receive.at[side, slot],
            lambda index: r.mix_send.at[side, index],
            y, up_y, down_y,
        )

    weights = [weight_ring(side) for side in range(2)]
    keys = [key_ring(side) for side in range(2)]
    mixes = [mix_ring(side) for side in range(2)]
    columns = Ring(
        (
            lambda slot: r.columns.at[core * 16 + slot],
            lambda slot: r.columns.at[(1 - core) * 16 + slot],
        ),
        lambda slot: r.column_receive.at[slot],
        lambda index: r.column_send.at[index],
        x, right, left,
        lambda slot: r.column_twin.at[slot],
        sibling,
    )

    def to_planes(ring):
        for e, device in zip(range(1, 4), planes):
            ring.push_far(0, 0, e, device)

    def turn_copy():
        place = (turn_seq // 2) % 4
        return remote(
            r.wo,
            r.columns.at[(turn_seq % 2) * 16 + place],
            r.column_send.at[31],
            r.column_receive.at[place],
            turned,
        )

    def normalize(part):
        loads[part].wait()

        def tile(index, carry):
            row = part * 128 + index * 16
            wide = r.raw[pl.ds(row, 16), :].astype(F32)
            mean_square = jnp.mean(wide * wide, axis=-1, keepdims=True)
            value = (wide * lax.rsqrt(mean_square + EPS) * r.gain[...]).astype(BF16)
            for chunk in range(16):
                r.normed[chunk, pl.ds(row, 16), :] = value[:, chunk * 256 : chunk * 256 + 256]
            return carry

        lax.fori_loop(0, 8, tile, 0)

    def reduced():
        def block(index, carry):
            rows = pl.ds(pl.multiple_of(index * 256, 256), 256)
            value = jnp.zeros((256, 192), F32)
            for chunk in range(16):
                value = value + dot_nt(
                    r.normed[chunk, rows, :], r.down_all[:, chunk * 256 : chunk * 256 + 256]
                )
            value = value.astype(BF16)
            for side in range(2):
                r.total[side, rows, :] = ADAPTER_SCALING * dot(value, r.up_all[side])
            return carry

        lax.fori_loop(0, 2, block, 0)

    def accumulate(side, d):
        ring = weights[side]
        for step in range(4):
            ring.handed(d, step)

        def block(index, carry):
            rows = pl.ds(pl.multiple_of(index * 256, 256), 256)
            value = r.total[side, rows, :]
            for step in range(4):
                chunk = ((z + 4 - d) % 4) * 4 + (x + step) % 4
                value = value + dot(
                    r.normed[chunk, rows, :], r.weights[side, ring.slot(d, step)]
                )
            r.total[side, rows, :] = value
            return carry

        lax.fori_loop(0, 2, block, 0)

    base = r.bases[pl.ds(seq, 1)]
    base_cos, base_sin = base[0, 0:1, :], base[0, 1:2, :]

    def project(side):
        ring = keys[side]
        for part in range(2):
            slot = ring.slot(part, 0)

            def tile(index, carry):
                rows = pl.ds(pl.multiple_of(part * 256 + index * 128, 128), 128)
                there = pl.ds(pl.multiple_of(index * 128, 128), 128)
                cos_row, sin_row = r.tables[0, rows, :], r.tables[1, rows, :]
                cos = cos_row * base_cos - sin_row * base_sin
                sin = sin_row * base_cos + cos_row * base_sin
                key = r.total[side, rows, 0:128]
                key = key * cos + pltpu.roll(key, 64, 1) * sin
                r.kv[side, core, slot, there, 0:128] = key.astype(BF16)
                r.kv[side, core, slot, there, 128:256] = r.total[side, rows, 128:256].astype(BF16)
                query = r.total[side, rows, 256:384]
                query = query * cos + pltpu.roll(query, 64, 1) * sin
                query = query * (math.log2(math.e) / math.sqrt(HD))
                r.q[side, rows, :] = query.astype(BF16)
                return carry

            lax.fori_loop(0, 2, tile, 0)
            ring.push_own(part)
            ring.push_far(part, 0, part + 2, planes[0])
            ring.hand(part, 0)

    def diagonal(side):
        for index in range(2):
            rows = pl.ds(index * 256, 256)
            pieces = []
            for part in range(index + 1):
                slot = keys[side].slot(part, 0)
                scores = dot_nt(r.q[side, rows, :], r.kv[side, core, slot, :, 0:128])
                if part == index:
                    row = lax.broadcasted_iota(jnp.int32, scores.shape, 0)
                    column = lax.broadcasted_iota(jnp.int32, scores.shape, 1)
                    scores = jnp.where(column <= row, scores, MASKED)
                pieces.append((slot, scores))
            highest = jnp.max(pieces[0][1], axis=1, keepdims=True)
            for slot, scores in pieces[1:]:
                highest = jnp.maximum(highest, jnp.max(scores, axis=1, keepdims=True))
            highest = jnp.broadcast_to(highest, (256, 128))
            value = jnp.zeros((256, 256), F32)
            for slot, scores in pieces:
                soft = jnp.exp2(scores - times(highest, 2)).astype(BF16)
                value = value + dot(soft, r.kv[side, core, slot, :, 128:384])
            r.top[rows, :] = highest
            r.mix[rows, :] = value

    def attend(side, places, bias):
        def block(index, carry):
            rows = pl.ds(pl.multiple_of(index * 256, 256), 256)
            query = r.q[side, rows, :]
            scores = [dot_nt(query, r.kv[side, which, slot, :, 0:128]) for which, slot in places]
            highest = scores[0]
            for value in scores[1:]:
                highest = jnp.maximum(highest, value)
            highest = jnp.max(highest, axis=1, keepdims=True)
            old = r.top[rows, :]
            new = jnp.maximum(old, highest + bias)
            level = times(new - bias, 2)
            value = r.mix[rows, :] * times(jnp.exp2(old - new), 2)
            for score, (which, slot) in zip(scores, places):
                soft = jnp.exp2(score - level).astype(BF16)
                value = value + dot(soft, r.kv[side, which, slot, :, 128:384])
            r.top[rows, :] = new
            r.mix[rows, :] = value
            return carry

        lax.fori_loop(0, 2, block, 0)

    def chip_places(side, d, step):
        slots = [keys[side].slot(d + part, step) for part in range(2)]
        return [(which, slot) for which in range(2) for slot in slots]

    def near(side):
        ring = keys[side]
        for part in range(2):
            ring.handed(part, 0)

        @pl.when(core == 1)
        def _():
            attend(side, [(0, ring.slot(part, 0)) for part in range(2)], 0.0)

    def own_plane(side, step):
        for part in range(2):
            keys[side].handed(part, step)

        @pl.when((x + step) % 4 < x)
        def _():
            attend(side, chip_places(side, 0, step), 0.0)

    def plane_before(side, step):
        for part in range(2):
            keys[side].handed(part + 2, step)
        flag = r.shifted[head * 2 + side]
        reaches = (z % 2) * (1 - flag) + (1 - z % 2) * flag
        bias = (reaches.astype(F32) - 1.0) * (-MASKED)
        attend(side, chip_places(side, 2, step), bias)

    def pass_on(side, d):
        keys[side].across(d)
        keys[side].push_far(d, 2, d + 2, planes[0])

    def close(side):
        ring = mixes[side]
        for part in range(2):
            rows = pl.ds(part * 256, 256)
            weight = r.mix[rows, 128:256]
            r.held[side, ring.slot(part, 0)] = (r.mix[rows, 0:128] / weight).astype(BF16)
            ring.push_far(part, 0, part + 2, partner)
            ring.push_own(part)
        for part in range(4):
            rows = pl.ds(part * 128, 128)
            sums = (r.top[rows, :] + jnp.log2(r.mix[rows, 128:256])) * math.log(2.0)
            r.sums_out[side : side + 1, part * 128 : part * 128 + 128] = sums.T[0:1, :]

    def add(side, d, step):
        rows = pl.ds((d % 2) * 256, 256)
        group = ((y + step) % 4) * 2 + (zh + d // 2) % 2
        block = r.held[side, mixes[side].slot(d, step)]
        behind = (z + 4 - group // 2) % 4
        first = behind * 4 + (group % 2) * 2
        rows_in = slice(side * 128, side * 128 + 128)
        matrix = jnp.concatenate(
            [r.columns[(j % 2) * 16 + first + j // 2, rows_in, :] for j in range(4)], axis=1
        )
        r.result[rows, :] += dot(block, matrix)
        lanes = pl.ds(pl.multiple_of(group * 256 + side * 128, 128), 128)
        r.low[rows, :] += dot_nt(block, r.down_o[:, lanes])

    w0, w1 = weights
    k0, k1 = keys
    m0, m1 = mixes
    to_planes(w0)
    w0.push_own(0)
    w0.hand(0, 0)

    @pl.when(jnp.logical_not(stays))
    def _():
        turn_copy().start()

    @pl.when(stays)
    def _():
        copy = pltpu.make_async_copy(
            r.wo, r.columns.at[(turn_seq % 2) * 16 + (turn_seq // 2) % 4], r.load.at[14]
        )
        copy.start()
        copy.wait()

    normalize(0)
    normalize(1)
    w0.own(1)
    w0.from_left(0)
    w0.from_right(0)
    normalize(2)
    normalize(3)
    w0.own(2)
    for copy in loads[4:]:
        copy.wait()
    reduced()
    w0.from_left(1)
    w0.from_right(1)
    w0.own(3)
    w0.across(0)
    accumulate(0, 0)
    to_planes(w1)
    w0.from_left(2)
    w0.from_right(2)
    w0.across(1)
    accumulate(0, 1)
    w0.from_left(3)
    w0.from_right(3)
    w1.push_own(0)
    w1.hand(0, 0)
    w1.own(1)
    w0.across(2)
    accumulate(0, 2)
    w1.own(2)
    w1.own(3)
    w0.across(3)
    accumulate(0, 3)
    project(0)

    for d in range(2):
        w1.from_left(d)
        w1.from_right(d)
    w1.across(0)
    accumulate(1, 0)
    for d in range(2, 4):
        w1.from_left(d)
        w1.from_right(d)
    w1.across(1)
    accumulate(1, 1)
    k0.from_left(0)
    k0.from_right(1)
    w1.across(2)
    accumulate(1, 2)
    w1.across(3)
    accumulate(1, 3)
    project(1)
    k0.from_left(1)
    k0.from_right(0)
    k0.own(2)
    k0.own(3)
    diagonal(0)
    near(0)
    own_plane(0, 3)
    pass_on(0, 0)
    pass_on(0, 1)
    k1.from_left(0)
    k1.from_right(1)
    own_plane(0, 1)
    plane_before(0, 0)
    own_plane(0, 2)
    k1.from_left(1)
    k1.from_right(0)
    k1.own(2)
    k1.own(3)
    for d in range(2, 4):
        k0.from_left(d, False)
        k0.from_right(d, False)
    plane_before(0, 3)
    plane_before(0, 1)
    pass_on(1, 0)
    pass_on(1, 1)
    k0.across(2)
    k0.across(3)
    plane_before(0, 2)
    close(0)

    @pl.when(jnp.logical_not(stays))
    def _():
        columns.arrived(0, 0)

    to_planes(columns)
    columns.hand(0, 0)
    diagonal(1)
    near(1)
    own_plane(1, 3)
    own_plane(1, 1)
    for d in range(2):
        m0.from_left(d)
        m0.from_right(d)
    own_plane(1, 2)
    plane_before(1, 0)
    columns.push_own(0)
    for d in range(1, 4):
        columns.own(d)
    for d in range(2, 4):
        k1.from_left(d, False)
        k1.from_right(d, False)
    m0.own(2)
    m0.own(3)
    plane_before(1, 3)
    plane_before(1, 1)
    k1.across(2)
    k1.across(3)
    plane_before(1, 2)
    close(1)

    for d in range(4):
        columns.from_left(d)
        columns.from_right(d)
    for d in range(2, 4):
        m0.from_left(d)
        m0.from_right(d)
    for d in range(2):
        m1.from_left(d)
        m1.from_right(d)
    for d in range(4):
        columns.across(d)
    r.result[...] = jnp.zeros_like(r.result)
    r.low[...] = jnp.zeros_like(r.low)
    for d in range(4):
        m0.across(d)
    m1.own(2)
    m1.own(3)
    for d in range(4):
        for step in range(4):
            columns.handed(d, step)
    for d in range(4):
        for step in range(4):
            add(0, d, step)
    for d in range(2):
        for step in (0, 1, 3):
            add(1, d, step)
    for d in range(2, 4):
        m1.from_left(d)
        m1.from_right(d)
    for d in range(2):
        m1.across(d)
        add(1, d, 2)
    for d in range(2, 4):
        for step in (0, 1, 3):
            add(1, d, step)
    for d in range(2, 4):
        m1.across(d)
        add(1, d, 2)
    r.out[...] = (
        r.result[...] + ADAPTER_SCALING * dot(r.low[...].astype(BF16), r.up_here[...])
    ).astype(BF16)
    for ring in weights + keys + mixes + [columns]:
        ring.finish()

    @pl.when(jnp.logical_not(stays))
    def _():
        turn_copy().wait_send()


def rope_tables():
    frequency = ROPE_BASE ** (-2.0 * np.arange(64, dtype=np.float64) / HD)
    sign = np.concatenate([-np.ones(64), np.ones(64)])

    def table(positions):
        angles = positions[:, None] * np.concatenate([frequency, frequency])[None, :]
        return np.cos(angles), np.sin(angles) * sign

    tables = np.stack(table(np.arange(TOK, dtype=np.float64)))
    bases = np.stack(table(np.arange(32, dtype=np.float64) * TOK), axis=1)
    return tables.astype(np.float32), bases.astype(np.float32)


VMEM = pl.BlockSpec(memory_space=pltpu.VMEM)
ANY = pl.BlockSpec(memory_space=pl.ANY)
SMEM = pl.BlockSpec(memory_space=pltpu.SMEM)


def body(
    activations,
    norm_gain,
    shifted,
    query_weight,
    key_weight,
    value_weight,
    output_weight,
    query_down,
    query_up,
    key_down,
    key_up,
    value_down,
    value_up,
    output_down,
    output_up_matrix,
):
    tables, bases = rope_tables()
    arguments = dict(
        act=(activations, ANY),
        gain=(norm_gain.reshape(1, D), VMEM),
        shifted=(shifted, SMEM),
        wq=(query_weight, VMEM),
        wk=(key_weight, VMEM),
        wv=(value_weight, VMEM),
        wo=(output_weight, VMEM),
        down_q=(query_down.T, ANY),
        up_q=(query_up, ANY),
        down_k=(key_down.T, ANY),
        up_k=(key_up, ANY),
        down_v=(value_down.T, ANY),
        up_v=(value_up, ANY),
        down_o=(output_down.T, VMEM),
        up_o=(output_up_matrix, ANY),
        tables=(jnp.asarray(tables), VMEM),
        bases=(jnp.asarray(bases), VMEM),
    )
    out, sums = pl.pallas_call(
        kernel,
        out_shape=(
            jax.ShapeDtypeStruct((TOK, 512), BF16),
            jax.ShapeDtypeStruct((2, TOK), F32),
        ),
        in_specs=[arguments[name][1] for name in INPUTS],
        out_specs=(VMEM, VMEM),
        scratch_shapes=list(SCRATCH.values()),
        compiler_params=pltpu.CompilerParams(
            collective_id=1, has_side_effects=True, vmem_limit_bytes=VMEM_BYTES
        ),
    )(*[arguments[name][0] for name in INPUTS])
    return out, sums.T


def solution(mesh):
    placed = (
        P("seq", None),
        P(),
        P(),
        P("seq", "head"),
        P("seq", "head"),
        P("seq", "head"),
        P("head", "seq"),
        P(),
        P(),
        P(),
        P(),
        P(),
        P(),
        P(),
        P(),
    )
    return jax.shard_map(
        body,
        mesh=mesh,
        in_specs=placed,
        out_specs=(P("seq", "head"), P("seq", "head")),
        check_vma=False,
    )
```

```python
import math

import jax
import jax.numpy as jnp
import numpy as np
from jax import lax
from jax.experimental import pallas as pl
from jax.experimental.pallas import tpu as pltpu
from jax.sharding import PartitionSpec as P

EPS = 1e-05
ADAPTER_SCALING = 0.5
ROPE_BASE = 10000.0
MASKED = -1e30
D = 4096
HD = 128
TOK = 512
MESH = pl.DeviceIdType.MESH
F32 = jnp.float32
BF16 = jnp.bfloat16
VMEM_BYTES = 56 * 1024 * 1024


def spot():
    seq = lax.axis_index("seq")
    head = lax.axis_index("head")
    return seq // 8, (seq // 2) % 4, seq % 2, head // 2, head % 2


def seq_of(z, x, core):
    return z * 8 + x * 2 + core


def remote(source, target, send, receive, device):
    return pltpu.make_async_remote_copy(
        src_ref=source,
        dst_ref=target,
        send_sem=send,
        recv_sem=receive,
        device_id=device,
        device_id_type=MESH,
    )


def dot(a, b):
    return jnp.dot(a, b, preferred_element_type=F32)


def dot_nt(a, b):
    return lax.dot_general(a, b, (((1,), (1,)), ((), ())), preferred_element_type=F32)


def times(value, n):
    return jnp.concatenate([value] * n, axis=1)


class Ring:
    def __init__(self, views, receive, send, place, right, left, twin=None, sibling=None):
        self.view, self.other = views
        self.receive, self.send = receive, send
        self.place, self.right, self.left = place, right, left
        self.twin, self.sibling = twin, sibling
        self.open = []

    def slot(self, d, step):
        return d * 4 + (self.place + step) % 4

    def start(self, source, target, receive, device):
        copy = remote(source, target, self.send(len(self.open)), receive, device)
        copy.start()
        self.open.append(copy)

    def push(self, d, step, device):
        slot = self.slot(d, step)
        self.start(self.view(slot), self.view(slot), self.receive(slot), device)

    def push_far(self, d, step, far, device):
        slot, there = self.slot(d, step), self.slot(far, step)
        self.start(self.view(slot), self.view(there), self.receive(there), device)

    def push_own(self, d):
        self.push(d, 0, self.right)
        self.push(d, 0, self.left)

    def hand(self, d, step):
        if self.sibling is not None:
            slot = self.slot(d, step)
            self.start(self.view(slot), self.view(slot), self.twin(slot), self.sibling)

    def handed(self, d, step):
        slot = self.slot(d, step)
        ref = self.other(slot)
        remote(ref, ref, self.send(0), self.twin(slot), self.sibling).wait_recv()

    def arrived(self, d, step):
        slot = self.slot(d, step)
        ref = self.view(slot)
        remote(ref, ref, self.send(0), self.receive(slot), self.right).wait_recv()

    def own(self, d):
        self.arrived(d, 0)
        self.push_own(d)
        self.hand(d, 0)

    def from_left(self, d, forward=True):
        self.arrived(d, 3)
        if forward and d % 2 == 0:
            self.push(d, 3, self.right)
        self.hand(d, 3)

    def from_right(self, d, forward=True):
        self.arrived(d, 1)
        if forward and d % 2 == 1:
            self.push(d, 1, self.left)
        self.hand(d, 1)

    def across(self, d):
        self.arrived(d, 2)
        self.hand(d, 2)

    def finish(self):
        for copy in self.open:
            copy.wait_send()


INPUTS = [
    "act",
    "gain",
    "shifted",
    "wq",
    "wk",
    "wv",
    "wo",
    "down_q",
    "up_q",
    "down_k",
    "up_k",
    "down_v",
    "up_v",
    "down_o",
    "up_o",
    "tables",
    "bases",
]
OUTPUTS = ["out", "sums_out"]
DMA = pltpu.SemaphoreType.DMA
SCRATCH = dict(
    raw=pltpu.VMEM((TOK, D), BF16),
    normed=pltpu.VMEM((16, TOK, 256), BF16),
    weights=pltpu.VMEM((16, 256, 768), BF16),
    down_all=pltpu.VMEM((192, D), BF16),
    up_all=pltpu.VMEM((192, 768), BF16),
    total=pltpu.VMEM((TOK, 768), F32),
    tables_here=pltpu.VMEM((2, TOK, HD), F32),
    down_here=pltpu.VMEM((64, 2048), BF16),
    q=pltpu.VMEM((2, TOK, HD), BF16),
    kv=pltpu.VMEM((2, 2, 16, 256, 384), BF16),
    top=pltpu.VMEM((TOK, 128), F32),
    mix=pltpu.VMEM((TOK, 256), F32),
    columns=pltpu.VMEM((32, 256, 128), BF16),
    held=pltpu.VMEM((2, 16, 256, 128), BF16),
    up_here=pltpu.VMEM((64, 512), BF16),
    low=pltpu.VMEM((TOK, 64), F32),
    result=pltpu.VMEM((TOK, 512), F32),
    load=DMA((23,)),
    weight_receive=DMA((3, 16)),
    weight_twin=DMA((3, 16)),
    weight_send=DMA((3, 31)),
    key_receive=DMA((2, 16)),
    key_twin=DMA((2, 16)),
    key_send=DMA((2, 30)),
    mix_receive=DMA((2, 16)),
    mix_send=DMA((2, 14)),
    column_receive=DMA((16,)),
    column_twin=DMA((16,)),
    column_send=DMA((32,)),
)


class Refs:
    pass


def kernel(*refs):
    r = Refs()
    for name, ref in zip(INPUTS + OUTPUTS + list(SCRATCH), refs):
        setattr(r, name, ref)
    z, x, core, y, zh = spot()
    seq = lax.axis_index("seq")
    head = lax.axis_index("head")
    sibling = (seq_of(z, x, 1 - core), head)
    right = (seq_of(z, (x + 1) % 4, core), head)
    left = (seq_of(z, (x + 3) % 4, core), head)
    planes = [(seq_of((z + e) % 4, x, core), head) for e in range(1, 4)]
    up_y = (seq, ((y + 1) % 4) * 2 + zh)
    down_y = (seq, ((y + 3) % 4) * 2 + zh)
    partner = (seq, y * 2 + 1 - zh)
    turn_seq = head * 4 + seq % 4
    turned = (turn_seq, seq // 4)
    stays = seq // 4 == head

    across_y = (seq, ((y + 2) % 4) * 2 + zh)
    barrier = pltpu.get_barrier_semaphore()
    everyone = [sibling, right, left, up_y, down_y, across_y, partner] + planes
    for device in everyone:
        pl.semaphore_signal(barrier, inc=1, device_id=device, device_id_type=MESH)

    @pl.when(jnp.logical_not(stays))
    def _():
        pl.semaphore_signal(barrier, inc=1, device_id=turned, device_id_type=MESH)

    own_rows = pl.ds(pl.multiple_of(core * 128, 128), 128)
    other_rows = pl.ds(pl.multiple_of(128 - core * 128, 128), 128)
    loads = []

    def load(source, target):
        copy = pltpu.make_async_copy(source, target, r.load.at[len(loads)])
        copy.start()
        loads.append(copy)

    places = {(0, 0): 0, (0, 1): 128, (1, 0): 256, (1, 1): 384, (0, 2): 512, (1, 2): 640}
    for (side, index), place in places.items():
        ref = (r.wk, r.wv, r.wq)[index]
        load(
            ref.at[:, pl.ds(side * 128, 128)],
            r.weights.at[x, own_rows, pl.ds(place, 128)],
        )
    for part in range(4):
        rows = pl.ds(part * 128, 128)
        load(r.act.at[rows], r.raw.at[rows])
    r.up_all[...] = jnp.zeros_like(r.up_all)
    for index, ref in enumerate((r.down_k, r.down_v, r.down_q)):
        load(ref, r.down_all.at[pl.ds(index * 64, 64)])
    for (side, index), place in places.items():
        here = pl.ds(pl.multiple_of(head * 256 + side * 128, 128), 128)
        ref = (r.up_k, r.up_v, r.up_q)[index]
        load(ref.at[:, here], r.up_all.at[pl.ds(index * 64, 64), pl.ds(place, 128)])
    load(r.tables, r.tables_here)
    load(r.up_o.at[:, pl.ds(pl.multiple_of(head * 512, 512), 512)], r.up_here)
    load(r.down_o, r.down_here)

    def ones(slot, carry):
        for side in range(2):
            for which in range(2):
                r.kv[side, which, slot, :, 256:384] = jnp.ones((256, 128), BF16)
        return carry

    lax.fori_loop(0, 16, ones, 0)

    def normalize(part):
        loads[6 + part].wait()

        def tile(index, carry):
            row = part * 128 + index * 16
            wide = r.raw[pl.ds(row, 16), :].astype(F32)
            mean_square = jnp.mean(wide * wide, axis=-1, keepdims=True)
            value = (wide * lax.rsqrt(mean_square + EPS) * r.gain[...]).astype(BF16)
            for chunk in range(16):
                r.normed[chunk, pl.ds(row, 16), :] = value[:, chunk * 256 : chunk * 256 + 256]
            return carry

        lax.fori_loop(0, 8, tile, 0)

    normalize(0)
    for copy in loads[:6]:
        copy.wait()
    pl.semaphore_wait(barrier, len(everyone) + 1 - stays.astype(jnp.int32))

    def weight_ring(side):
        return Ring(
            (
                lambda slot: r.weights.at[slot, own_rows, pl.ds(side * 256, 256)],
                lambda slot: r.weights.at[slot, other_rows, pl.ds(side * 256, 256)],
            ),
            lambda slot: r.weight_receive.at[side, slot],
            lambda index: r.weight_send.at[side, index],
            x, right, left,
            lambda slot: r.weight_twin.at[side, slot],
            sibling,
        )

    def key_ring(side):
        return Ring(
            (
                lambda slot: r.kv.at[side, core, slot, :, pl.ds(0, 256)],
                lambda slot: r.kv.at[side, 1 - core, slot, :, pl.ds(0, 256)],
            ),
            lambda slot: r.key_receive.at[side, slot],
            lambda index: r.key_send.at[side, index],
            x, right, left,
            lambda slot: r.key_twin.at[side, slot],
            sibling,
        )

    def mix_ring(side):
        return Ring(
            (lambda slot: r.held.at[side, slot], None),
            lambda slot: r.mix_receive.at[side, slot],
            lambda index: r.mix_send.at[side, index],
            y, up_y, down_y,
        )

    weights = [weight_ring(side) for side in range(3)]
    keys = [key_ring(side) for side in range(2)]
    mixes = [mix_ring(side) for side in range(2)]
    columns = Ring(
        (
            lambda slot: r.columns.at[core * 16 + slot],
            lambda slot: r.columns.at[(1 - core) * 16 + slot],
        ),
        lambda slot: r.column_receive.at[slot],
        lambda index: r.column_send.at[index],
        x, right, left,
        lambda slot: r.column_twin.at[slot],
        sibling,
    )

    def to_planes(ring):
        for e, device in zip(range(1, 4), planes):
            ring.push_far(0, 0, e, device)

    def turn_copy():
        place = (turn_seq // 2) % 4
        return remote(
            r.wo,
            r.columns.at[(turn_seq % 2) * 16 + place],
            r.column_send.at[31],
            r.column_receive.at[place],
            turned,
        )

    def reduced():
        every = jnp.concatenate([r.normed[chunk] for chunk in range(16)], axis=1)
        value = dot_nt(every, r.down_all[...]).astype(BF16)
        r.total[...] = ADAPTER_SCALING * dot(value, r.up_all[...])

    def accumulate(side, d):
        ring = weights[side]
        for step in range(4):
            ring.handed(d, step)
        chunks = [((z + 4 - d) % 4) * 4 + (x + step) % 4 for step in range(4)]
        left_side = jnp.concatenate([r.normed[chunk] for chunk in chunks], axis=1)
        lanes = slice(side * 256, side * 256 + 256)
        matrix = jnp.concatenate(
            [r.weights[ring.slot(d, step), :, lanes] for step in range(4)], axis=0
        )
        r.total[:, lanes] += dot(left_side, matrix)

    base = r.bases[pl.ds(seq, 1)]
    base_cos, base_sin = base[0, 0:1, :], base[0, 1:2, :]

    def turned_rows(rows, value):
        cos_row, sin_row = r.tables_here[0, rows, :], r.tables_here[1, rows, :]
        cos = cos_row * base_cos - sin_row * base_sin
        sin = sin_row * base_cos + cos_row * base_sin
        return value * cos + pltpu.roll(value, 64, 1) * sin

    def project_keys(side):
        ring = keys[side]
        for part in range(2):
            slot = ring.slot(part, 0)
            rows = pl.ds(part * 256, 256)
            key = turned_rows(rows, r.total[rows, side * 256 : side * 256 + 128])
            r.kv[side, core, slot, :, 0:128] = key.astype(BF16)
            value = r.total[rows, side * 256 + 128 : side * 256 + 256]
            r.kv[side, core, slot, :, 128:256] = value.astype(BF16)
            ring.push_own(part)
            ring.push_far(part, 0, part + 2, planes[0])
            ring.hand(part, 0)

    def project_queries(side):
        for part in range(4):
            rows = pl.ds(part * 128, 128)
            query = turned_rows(rows, r.total[rows, 512 + side * 128 : 640 + side * 128])
            query = query * (math.log2(math.e) / math.sqrt(HD))
            r.q[side, rows, :] = query.astype(BF16)

    def diagonal(side):
        for index in range(2):
            rows = pl.ds(index * 256, 256)
            pieces = []
            for part in range(index + 1):
                slot = keys[side].slot(part, 0)
                scores = dot_nt(r.q[side, rows, :], r.kv[side, core, slot, :, 0:128])
                if part == index:
                    row = lax.broadcasted_iota(jnp.int32, scores.shape, 0)
                    column = lax.broadcasted_iota(jnp.int32, scores.shape, 1)
                    scores = jnp.where(column <= row, scores, MASKED)
                pieces.append((slot, scores))
            highest = jnp.max(pieces[0][1], axis=1, keepdims=True)
            for slot, scores in pieces[1:]:
                highest = jnp.maximum(highest, jnp.max(scores, axis=1, keepdims=True))
            highest = jnp.broadcast_to(highest, (256, 128))
            value = jnp.zeros((256, 256), F32)
            for slot, scores in pieces:
                soft = jnp.exp2(scores - times(highest, 2)).astype(BF16)
                value = value + dot(soft, r.kv[side, core, slot, :, 128:384])
            r.top[rows, :] = highest
            r.mix[rows, :] = value

    def attend(side, places, bias):
        key = jnp.concatenate([r.kv[side, which, slot, :, 0:128] for which, slot in places], axis=0)
        value = jnp.concatenate(
            [r.kv[side, which, slot, :, 128:384] for which, slot in places], axis=0
        )
        for index in range(4):
            rows = pl.ds(index * 128, 128)
            scores = dot_nt(r.q[side, rows, :], key)
            old = r.top[rows, :]
            new = jnp.maximum(old, jnp.max(scores, axis=1, keepdims=True) + bias)
            soft = jnp.exp2(scores - times(new - bias, 2 * len(places))).astype(BF16)
            r.mix[rows, :] = r.mix[rows, :] * times(jnp.exp2(old - new), 2) + dot(soft, value)
            r.top[rows, :] = new

    def chip_places(side, d, step):
        slots = [keys[side].slot(d + part, step) for part in range(2)]
        return [(which, slot) for which in range(2) for slot in slots]

    def near(side):
        ring = keys[side]
        for part in range(2):
            ring.handed(part, 0)

        @pl.when(core == 1)
        def _():
            attend(side, [(0, ring.slot(part, 0)) for part in range(2)], 0.0)

    def own_plane(side, step):
        for part in range(2):
            keys[side].handed(part, step)

        @pl.when((x + step) % 4 < x)
        def _():
            attend(side, chip_places(side, 0, step), 0.0)

    def plane_before(side, step):
        for part in range(2):
            keys[side].handed(part + 2, step)
        flag = r.shifted[head * 2 + side]
        reaches = (z % 2) * (1 - flag) + (1 - z % 2) * flag
        bias = (reaches.astype(F32) - 1.0) * (-MASKED)
        attend(side, chip_places(side, 2, step), bias)

    def pass_on(side, d):
        keys[side].across(d)
        keys[side].push_far(d, 2, d + 2, planes[0])

    def push_mixed(side, d):
        for device in (up_y, down_y, across_y):
            mixes[side].push(d, 0, device)

    def close(side):
        ring = mixes[side]
        for part in range(2):
            rows = pl.ds(part * 256, 256)
            weight = r.mix[rows, 128:256]
            r.held[side, ring.slot(part, 0)] = (r.mix[rows, 0:128] / weight).astype(BF16)
            ring.push_far(part, 0, part + 2, partner)
        for part in range(2):
            push_mixed(side, part)
        for part in range(4):
            rows = pl.ds(part * 128, 128)
            sums = (r.top[rows, :] + jnp.log2(r.mix[rows, 128:256])) * math.log(2.0)
            r.sums_out[side : side + 1, part * 128 : part * 128 + 128] = sums.T[0:1, :]

    def add(side, d):
        rows = pl.ds((d % 2) * 256, 256)
        groups = [((y + step) % 4) * 2 + (zh + d // 2) % 2 for step in range(4)]
        slots = [mixes[side].slot(d, step) for step in range(4)]
        block = jnp.concatenate([r.held[side, slot] for slot in slots], axis=1)
        rows_in = slice(side * 128, side * 128 + 128)
        matrix = []
        down = []
        for group in groups:
            first = ((z + 4 - group // 2) % 4) * 4 + (group % 2) * 2
            matrix.append(
                jnp.concatenate(
                    [r.columns[(j % 2) * 16 + first + j // 2, rows_in, :] for j in range(4)],
                    axis=1,
                )
            )
            lanes = pl.ds(pl.multiple_of(group * 256 + side * 128, 128), 128)
            down.append(r.down_here[:, lanes])
        r.result[rows, :] += dot(block, jnp.concatenate(matrix, axis=0))
        r.low[rows, :] += dot_nt(block, jnp.concatenate(down, axis=1))

    w0, w1, w2 = weights
    k0, k1 = keys
    m0, m1 = mixes
    to_planes(w0)
    for ring in weights:
        ring.push_own(0)
        ring.hand(0, 0)
    normalize(1)
    w0.from_left(0)
    w0.from_right(0)
    to_planes(w1)
    w0.own(1)
    normalize(2)
    w0.own(2)
    w1.from_left(0)
    w1.from_right(0)
    w0.own(3)
    to_planes(w2)
    normalize(3)
    w0.from_left(1)
    w0.from_right(1)
    w0.from_left(2)
    w0.from_right(2)
    for copy in loads[10:]:
        copy.wait()
    reduced()
    w0.from_left(3)
    w0.from_right(3)
    w2.from_left(0)
    w2.from_right(0)
    for d in range(1, 4):
        w1.own(d)

    @pl.when(jnp.logical_not(stays))
    def _():
        turn_copy().start()

    @pl.when(stays)
    def _():
        copy = pltpu.make_async_copy(
            r.wo, r.columns.at[(turn_seq % 2) * 16 + (turn_seq // 2) % 4], r.load.at[22]
        )
        copy.start()
        copy.wait()

    for d in range(4):
        w0.across(d)
        accumulate(0, d)
    project_keys(0)
    for d in range(1, 4):
        w1.from_left(d)
        w1.from_right(d)
    for d in range(1, 4):
        w2.own(d)
    k0.from_left(0)
    k0.from_right(1)
    for d in range(4):
        w1.across(d)
        accumulate(1, d)
    k0.from_left(1)
    k0.from_right(0)
    k0.own(2)
    k0.own(3)
    for d in range(1, 4):
        w2.from_left(d)
        w2.from_right(d)
    pass_on(0, 0)
    pass_on(0, 1)
    project_keys(1)

    @pl.when(jnp.logical_not(stays))
    def _():
        columns.arrived(0, 0)

    columns.hand(0, 0)
    to_planes(columns)
    for d in range(4):
        w2.across(d)
        accumulate(2, d)
    project_queries(0)
    project_queries(1)

    diagonal(0)
    near(0)
    own_plane(0, 3)
    own_plane(0, 1)
    own_plane(0, 2)
    plane_before(0, 0)
    k1.from_left(0)
    k1.from_right(1)
    for d in range(2, 4):
        k0.from_left(d, False)
        k0.from_right(d, False)
    plane_before(0, 3)
    plane_before(0, 1)
    k1.from_left(1)
    k1.from_right(0)
    k1.own(2)
    k1.own(3)
    k0.across(2)
    k0.across(3)
    pass_on(1, 0)
    pass_on(1, 1)
    columns.push_own(0)
    for d in range(1, 4):
        columns.own(d)
    plane_before(0, 2)
    close(0)

    diagonal(1)
    near(1)
    own_plane(1, 3)
    own_plane(1, 1)
    own_plane(1, 2)
    plane_before(1, 0)
    for d in range(2, 4):
        k1.from_left(d, False)
        k1.from_right(d, False)
    plane_before(1, 3)
    plane_before(1, 1)
    for d in range(2, 4):
        m0.arrived(d, 0)
        push_mixed(0, d)
    k1.across(2)
    k1.across(3)
    plane_before(1, 2)
    close(1)

    for d in range(4):
        columns.from_left(d)
        columns.from_right(d)
    r.result[...] = jnp.zeros_like(r.result)
    r.low[...] = jnp.zeros_like(r.low)
    for d in range(2, 4):
        m1.arrived(d, 0)
        push_mixed(1, d)
    for d in range(4):
        columns.across(d)
    for d in range(4):
        for step in range(4):
            columns.handed(d, step)
    for d in range(4):
        for step in range(1, 4):
            m0.arrived(d, step)
        add(0, d)
    for d in range(4):
        for step in range(1, 4):
            m1.arrived(d, step)
        add(1, d)
    r.out[...] = (
        r.result[...] + ADAPTER_SCALING * dot(r.low[...].astype(BF16), r.up_here[...])
    ).astype(BF16)
    for ring in weights + keys + mixes + [columns]:
        ring.finish()

    @pl.when(jnp.logical_not(stays))
    def _():
        turn_copy().wait_send()


def rope_tables():
    frequency = ROPE_BASE ** (-2.0 * np.arange(64, dtype=np.float64) / HD)
    sign = np.concatenate([-np.ones(64), np.ones(64)])

    def table(positions):
        angles = positions[:, None] * np.concatenate([frequency, frequency])[None, :]
        return np.cos(angles), np.sin(angles) * sign

    tables = np.stack(table(np.arange(TOK, dtype=np.float64)))
    bases = np.stack(table(np.arange(32, dtype=np.float64) * TOK), axis=1)
    return tables.astype(np.float32), bases.astype(np.float32)


VMEM = pl.BlockSpec(memory_space=pltpu.VMEM)
ANY = pl.BlockSpec(memory_space=pl.ANY)
SMEM = pl.BlockSpec(memory_space=pltpu.SMEM)


def body(
    activations,
    norm_gain,
    shifted,
    query_weight,
    key_weight,
    value_weight,
    output_weight,
    query_down,
    query_up,
    key_down,
    key_up,
    value_down,
    value_up,
    output_down,
    output_up_matrix,
):
    tables, bases = rope_tables()
    arguments = dict(
        act=(activations, ANY),
        gain=(norm_gain.reshape(1, D), VMEM),
        shifted=(shifted, SMEM),
        wq=(query_weight, ANY),
        wk=(key_weight, ANY),
        wv=(value_weight, ANY),
        wo=(output_weight, ANY),
        down_q=(query_down.T, ANY),
        up_q=(query_up, ANY),
        down_k=(key_down.T, ANY),
        up_k=(key_up, ANY),
        down_v=(value_down.T, ANY),
        up_v=(value_up, ANY),
        down_o=(output_down.T, ANY),
        up_o=(output_up_matrix, ANY),
        tables=(jnp.asarray(tables), ANY),
        bases=(jnp.asarray(bases), VMEM),
    )
    out, sums = pl.pallas_call(
        kernel,
        out_shape=(
            jax.ShapeDtypeStruct((TOK, 512), BF16),
            jax.ShapeDtypeStruct((2, TOK), F32),
        ),
        in_specs=[arguments[name][1] for name in INPUTS],
        out_specs=(VMEM, VMEM),
        scratch_shapes=list(SCRATCH.values()),
        compiler_params=pltpu.CompilerParams(
            collective_id=1, has_side_effects=True, vmem_limit_bytes=VMEM_BYTES
        ),
    )(*[arguments[name][0] for name in INPUTS])
    return out, sums.T


def solution(mesh):
    placed = (
        P("seq", None),
        P(),
        P(),
        P("seq", "head"),
        P("seq", "head"),
        P("seq", "head"),
        P("head", "seq"),
        P(),
        P(),
        P(),
        P(),
        P(),
        P(),
        P(),
        P(),
    )
    return jax.shard_map(
        body,
        mesh=mesh,
        in_specs=placed,
        out_specs=(P("seq", "head"), P("seq", "head")),
        check_vma=False,
    )
```

```python
import math

import jax
import jax.numpy as jnp
import numpy as np
from jax import lax
from jax.experimental import pallas as pl
from jax.experimental.pallas import tpu as pltpu
from jax.sharding import PartitionSpec as P

EPS = 1e-05
ADAPTER_SCALING = 0.5
ROPE_BASE = 10000.0
MASKED = -1e30
D = 4096
HD = 128
TOK = 512
MESH = pl.DeviceIdType.MESH
F32 = jnp.float32
BF16 = jnp.bfloat16
VMEM_BYTES = 56 * 1024 * 1024


def spot():
    seq = lax.axis_index("seq")
    head = lax.axis_index("head")
    return seq // 8, (seq // 2) % 4, seq % 2, head // 2, head % 2


def seq_of(z, x, core):
    return z * 8 + x * 2 + core


def remote(source, target, send, receive, device):
    return pltpu.make_async_remote_copy(
        src_ref=source,
        dst_ref=target,
        send_sem=send,
        recv_sem=receive,
        device_id=device,
        device_id_type=MESH,
    )


def dot(a, b):
    return jnp.dot(a, b, preferred_element_type=F32)


def dot_nt(a, b):
    return lax.dot_general(a, b, (((1,), (1,)), ((), ())), preferred_element_type=F32)


def times(value, n):
    return jnp.concatenate([value] * n, axis=1)


class Ring:
    def __init__(self, views, receive, send, place, right, left, twin=None, sibling=None):
        self.view, self.other = views
        self.receive, self.send = receive, send
        self.place, self.right, self.left = place, right, left
        self.twin, self.sibling = twin, sibling
        self.open = []

    def slot(self, d, step):
        return d * 4 + (self.place + step) % 4

    def start(self, source, target, receive, device):
        copy = remote(source, target, self.send(len(self.open)), receive, device)
        copy.start()
        self.open.append(copy)

    def push(self, d, step, device):
        slot = self.slot(d, step)
        self.start(self.view(slot), self.view(slot), self.receive(slot), device)

    def push_far(self, d, step, far, device):
        slot, there = self.slot(d, step), self.slot(far, step)
        self.start(self.view(slot), self.view(there), self.receive(there), device)

    def push_own(self, d):
        self.push(d, 0, self.right)
        self.push(d, 0, self.left)

    def hand(self, d, step):
        if self.sibling is not None:
            slot = self.slot(d, step)
            self.start(self.view(slot), self.view(slot), self.twin(slot), self.sibling)

    def handed(self, d, step):
        slot = self.slot(d, step)
        ref = self.other(slot)
        remote(ref, ref, self.send(0), self.twin(slot), self.sibling).wait_recv()

    def arrived(self, d, step):
        slot = self.slot(d, step)
        ref = self.view(slot)
        remote(ref, ref, self.send(0), self.receive(slot), self.right).wait_recv()

    def own(self, d):
        self.arrived(d, 0)
        self.push_own(d)
        self.hand(d, 0)

    def from_left(self, d, forward=True):
        self.arrived(d, 3)
        if forward and d % 2 == 0:
            self.push(d, 3, self.right)
        self.hand(d, 3)

    def from_right(self, d, forward=True):
        self.arrived(d, 1)
        if forward and d % 2 == 1:
            self.push(d, 1, self.left)
        self.hand(d, 1)

    def across(self, d):
        self.arrived(d, 2)
        self.hand(d, 2)

    def finish(self):
        for copy in self.open:
            copy.wait_send()


INPUTS = [
    "act",
    "gain",
    "shifted",
    "wq",
    "wk",
    "wv",
    "wo",
    "down_q",
    "up_q",
    "down_k",
    "up_k",
    "down_v",
    "up_v",
    "down_o",
    "up_o",
    "tables",
    "bases",
]
OUTPUTS = ["out", "sums_out"]
DMA = pltpu.SemaphoreType.DMA
SCRATCH = dict(
    raw=pltpu.VMEM((TOK, D), BF16),
    normed=pltpu.VMEM((16, TOK, 256), BF16),
    weights=pltpu.VMEM((16, 256, 768), BF16),
    down_all=pltpu.VMEM((192, D), BF16),
    up_all=pltpu.VMEM((192, 768), BF16),
    total=pltpu.VMEM((TOK, 768), F32),
    tables_here=pltpu.VMEM((2, TOK, HD), F32),
    down_here=pltpu.VMEM((64, 2048), BF16),
    q=pltpu.VMEM((2, TOK, HD), BF16),
    kv=pltpu.VMEM((2, 2, 16, 256, 384), BF16),
    top=pltpu.VMEM((TOK, 128), F32),
    mix=pltpu.VMEM((TOK, 256), F32),
    columns=pltpu.VMEM((32, 256, 128), BF16),
    held=pltpu.VMEM((2, 16, 256, 128), BF16),
    up_here=pltpu.VMEM((64, 512), BF16),
    low=pltpu.VMEM((TOK, 64), F32),
    result=pltpu.VMEM((TOK, 512), F32),
    load=DMA((23,)),
    weight_receive=DMA((3, 16)),
    weight_twin=DMA((3, 16)),
    weight_send=DMA((3, 31)),
    key_receive=DMA((2, 16)),
    key_twin=DMA((2, 16)),
    key_send=DMA((2, 30)),
    mix_receive=DMA((2, 16)),
    mix_send=DMA((2, 14)),
    column_receive=DMA((16,)),
    column_twin=DMA((16,)),
    column_send=DMA((32,)),
)


class Refs:
    pass


def kernel(*refs):
    r = Refs()
    for name, ref in zip(INPUTS + OUTPUTS + list(SCRATCH), refs):
        setattr(r, name, ref)
    z, x, core, y, zh = spot()
    seq = lax.axis_index("seq")
    head = lax.axis_index("head")
    sibling = (seq_of(z, x, 1 - core), head)
    right = (seq_of(z, (x + 1) % 4, core), head)
    left = (seq_of(z, (x + 3) % 4, core), head)
    planes = [(seq_of((z + e) % 4, x, core), head) for e in range(1, 4)]
    up_y = (seq, ((y + 1) % 4) * 2 + zh)
    down_y = (seq, ((y + 3) % 4) * 2 + zh)
    partner = (seq, y * 2 + 1 - zh)
    turn_seq = head * 4 + seq % 4
    turned = (turn_seq, seq // 4)
    stays = seq // 4 == head

    across_y = (seq, ((y + 2) % 4) * 2 + zh)
    barrier = pltpu.get_barrier_semaphore()
    everyone = [sibling, right, left, up_y, down_y, across_y, partner] + planes
    for device in everyone:
        pl.semaphore_signal(barrier, inc=1, device_id=device, device_id_type=MESH)

    @pl.when(jnp.logical_not(stays))
    def _():
        pl.semaphore_signal(barrier, inc=1, device_id=turned, device_id_type=MESH)

    own_rows = pl.ds(pl.multiple_of(core * 128, 128), 128)
    other_rows = pl.ds(pl.multiple_of(128 - core * 128, 128), 128)
    loads = []

    def load(source, target):
        copy = pltpu.make_async_copy(source, target, r.load.at[len(loads)])
        copy.start()
        loads.append(copy)

    places = {(0, 0): 0, (0, 1): 128, (1, 0): 256, (1, 1): 384, (0, 2): 512, (1, 2): 640}
    for (side, index), place in places.items():
        ref = (r.wk, r.wv, r.wq)[index]
        load(
            ref.at[:, pl.ds(side * 128, 128)],
            r.weights.at[x, own_rows, pl.ds(place, 128)],
        )
    for part in range(4):
        rows = pl.ds(part * 128, 128)
        load(r.act.at[rows], r.raw.at[rows])
    r.up_all[...] = jnp.zeros_like(r.up_all)
    for index, ref in enumerate((r.down_k, r.down_v, r.down_q)):
        load(ref, r.down_all.at[pl.ds(index * 64, 64)])
    for (side, index), place in places.items():
        here = pl.ds(pl.multiple_of(head * 256 + side * 128, 128), 128)
        ref = (r.up_k, r.up_v, r.up_q)[index]
        load(ref.at[:, here], r.up_all.at[pl.ds(index * 64, 64), pl.ds(place, 128)])
    load(r.tables, r.tables_here)
    load(r.up_o.at[:, pl.ds(pl.multiple_of(head * 512, 512), 512)], r.up_here)
    load(r.down_o, r.down_here)

    def ones(slot, carry):
        for side in range(2):
            for which in range(2):
                r.kv[side, which, slot, :, 256:384] = jnp.ones((256, 128), BF16)
        return carry

    lax.fori_loop(0, 16, ones, 0)

    def normalize(part):
        loads[6 + part].wait()

        def tile(index, carry):
            row = part * 128 + index * 16
            wide = r.raw[pl.ds(row, 16), :].astype(F32)
            mean_square = jnp.mean(wide * wide, axis=-1, keepdims=True)
            value = (wide * lax.rsqrt(mean_square + EPS) * r.gain[...]).astype(BF16)
            for chunk in range(16):
                r.normed[chunk, pl.ds(row, 16), :] = value[:, chunk * 256 : chunk * 256 + 256]
            return carry

        lax.fori_loop(0, 8, tile, 0)

    normalize(0)
    for copy in loads[:6]:
        copy.wait()
    pl.semaphore_wait(barrier, len(everyone) + 1 - stays.astype(jnp.int32))

    def weight_ring(side):
        return Ring(
            (
                lambda slot: r.weights.at[slot, own_rows, pl.ds(side * 256, 256)],
                lambda slot: r.weights.at[slot, other_rows, pl.ds(side * 256, 256)],
            ),
            lambda slot: r.weight_receive.at[side, slot],
            lambda index: r.weight_send.at[side, index],
            x, right, left,
            lambda slot: r.weight_twin.at[side, slot],
            sibling,
        )

    def key_ring(side):
        return Ring(
            (
                lambda slot: r.kv.at[side, core, slot, :, pl.ds(0, 256)],
                lambda slot: r.kv.at[side, 1 - core, slot, :, pl.ds(0, 256)],
            ),
            lambda slot: r.key_receive.at[side, slot],
            lambda index: r.key_send.at[side, index],
            x, right, left,
            lambda slot: r.key_twin.at[side, slot],
            sibling,
        )

    def mix_ring(side):
        return Ring(
            (lambda slot: r.held.at[side, slot], None),
            lambda slot: r.mix_receive.at[side, slot],
            lambda index: r.mix_send.at[side, index],
            y, up_y, down_y,
        )

    weights = [weight_ring(side) for side in range(3)]
    keys = [key_ring(side) for side in range(2)]
    mixes = [mix_ring(side) for side in range(2)]
    columns = Ring(
        (
            lambda slot: r.columns.at[core * 16 + slot],
            lambda slot: r.columns.at[(1 - core) * 16 + slot],
        ),
        lambda slot: r.column_receive.at[slot],
        lambda index: r.column_send.at[index],
        x, right, left,
        lambda slot: r.column_twin.at[slot],
        sibling,
    )

    def to_planes(ring):
        for e, device in zip(range(1, 4), planes):
            ring.push_far(0, 0, e, device)

    def turn_copy():
        place = (turn_seq // 2) % 4
        return remote(
            r.wo,
            r.columns.at[(turn_seq % 2) * 16 + place],
            r.column_send.at[31],
            r.column_receive.at[place],
            turned,
        )

    def reduced():
        every = jnp.concatenate([r.normed[chunk] for chunk in range(16)], axis=1)
        value = dot_nt(every, r.down_all[...]).astype(BF16)
        r.total[...] = ADAPTER_SCALING * dot(value, r.up_all[...])

    def accumulate(side, d):
        ring = weights[side]
        for step in range(4):
            ring.handed(d, step)
        chunks = [((z + 4 - d) % 4) * 4 + (x + step) % 4 for step in range(4)]
        left_side = jnp.concatenate([r.normed[chunk] for chunk in chunks], axis=1)
        lanes = slice(side * 256, side * 256 + 256)
        matrix = jnp.concatenate(
            [r.weights[ring.slot(d, step), :, lanes] for step in range(4)], axis=0
        )
        r.total[:, lanes] += dot(left_side, matrix)

    base = r.bases[pl.ds(seq, 1)]
    base_cos, base_sin = base[0, 0:1, :], base[0, 1:2, :]

    def turned_rows(rows, value):
        cos_row, sin_row = r.tables_here[0, rows, :], r.tables_here[1, rows, :]
        cos = cos_row * base_cos - sin_row * base_sin
        sin = sin_row * base_cos + cos_row * base_sin
        return value * cos + pltpu.roll(value, 64, 1) * sin

    def project_keys(side):
        ring = keys[side]
        for part in range(2):
            slot = ring.slot(part, 0)
            rows = pl.ds(part * 256, 256)
            key = turned_rows(rows, r.total[rows, side * 256 : side * 256 + 128])
            r.kv[side, core, slot, :, 0:128] = key.astype(BF16)
            value = r.total[rows, side * 256 + 128 : side * 256 + 256]
            r.kv[side, core, slot, :, 128:256] = value.astype(BF16)
            ring.push_own(part)
            ring.push_far(part, 0, part + 2, planes[0])
            ring.hand(part, 0)

    def project_queries(side):
        for part in range(4):
            rows = pl.ds(part * 128, 128)
            query = turned_rows(rows, r.total[rows, 512 + side * 128 : 640 + side * 128])
            query = query * (math.log2(math.e) / math.sqrt(HD))
            r.q[side, rows, :] = query.astype(BF16)

    def diagonal(side):
        for index in range(2):
            rows = pl.ds(index * 256, 256)
            pieces = []
            for part in range(index + 1):
                slot = keys[side].slot(part, 0)
                scores = dot_nt(r.q[side, rows, :], r.kv[side, core, slot, :, 0:128])
                if part == index:
                    row = lax.broadcasted_iota(jnp.int32, scores.shape, 0)
                    column = lax.broadcasted_iota(jnp.int32, scores.shape, 1)
                    scores = jnp.where(column <= row, scores, MASKED)
                pieces.append((slot, scores))
            highest = jnp.max(pieces[0][1], axis=1, keepdims=True)
            for slot, scores in pieces[1:]:
                highest = jnp.maximum(highest, jnp.max(scores, axis=1, keepdims=True))
            highest = jnp.broadcast_to(highest, (256, 128))
            value = jnp.zeros((256, 256), F32)
            for slot, scores in pieces:
                soft = jnp.exp2(scores - times(highest, 2)).astype(BF16)
                value = value + dot(soft, r.kv[side, core, slot, :, 128:384])
            r.top[rows, :] = highest
            r.mix[rows, :] = value

    def attend(side, places, bias):
        key = jnp.concatenate([r.kv[side, which, slot, :, 0:128] for which, slot in places], axis=0)
        value = jnp.concatenate(
            [r.kv[side, which, slot, :, 128:384] for which, slot in places], axis=0
        )
        for index in range(4):
            rows = pl.ds(index * 128, 128)
            scores = dot_nt(r.q[side, rows, :], key)
            old = r.top[rows, :]
            new = jnp.maximum(old, jnp.max(scores, axis=1, keepdims=True) + bias)
            soft = jnp.exp2(scores - times(new - bias, 2 * len(places))).astype(BF16)
            r.mix[rows, :] = r.mix[rows, :] * times(jnp.exp2(old - new), 2) + dot(soft, value)
            r.top[rows, :] = new

    def chip_places(side, d, step):
        slots = [keys[side].slot(d + part, step) for part in range(2)]
        return [(which, slot) for which in range(2) for slot in slots]

    def near(side):
        ring = keys[side]
        for part in range(2):
            ring.handed(part, 0)

        @pl.when(core == 1)
        def _():
            attend(side, [(0, ring.slot(part, 0)) for part in range(2)], 0.0)

    def own_plane(side, step):
        for part in range(2):
            keys[side].handed(part, step)

        @pl.when((x + step) % 4 < x)
        def _():
            attend(side, chip_places(side, 0, step), 0.0)

    def plane_before(side, step):
        for part in range(2):
            keys[side].handed(part + 2, step)
        flag = r.shifted[head * 2 + side]
        reaches = (z % 2) * (1 - flag) + (1 - z % 2) * flag
        bias = (reaches.astype(F32) - 1.0) * (-MASKED)
        attend(side, chip_places(side, 2, step), bias)

    def pass_on(side, d):
        keys[side].across(d)
        keys[side].push_far(d, 2, d + 2, planes[0])

    def push_mixed(side, d):
        for device in (up_y, down_y, across_y):
            mixes[side].push(d, 0, device)

    def close(side):
        ring = mixes[side]
        for part in range(2):
            rows = pl.ds(part * 256, 256)
            weight = r.mix[rows, 128:256]
            r.held[side, ring.slot(part, 0)] = (r.mix[rows, 0:128] / weight).astype(BF16)
            ring.push_far(part, 0, part + 2, partner)
        for part in range(2):
            push_mixed(side, part)
        for part in range(4):
            rows = pl.ds(part * 128, 128)
            sums = (r.top[rows, :] + jnp.log2(r.mix[rows, 128:256])) * math.log(2.0)
            r.sums_out[side : side + 1, part * 128 : part * 128 + 128] = sums.T[0:1, :]

    def add(side, d):
        rows = pl.ds((d % 2) * 256, 256)
        groups = [((y + step) % 4) * 2 + (zh + d // 2) % 2 for step in range(4)]
        slots = [mixes[side].slot(d, step) for step in range(4)]
        block = jnp.concatenate([r.held[side, slot] for slot in slots], axis=1)
        rows_in = slice(side * 128, side * 128 + 128)
        matrix = []
        down = []
        for group in groups:
            first = ((z + 4 - group // 2) % 4) * 4 + (group % 2) * 2
            matrix.append(
                jnp.concatenate(
                    [r.columns[(j % 2) * 16 + first + j // 2, rows_in, :] for j in range(4)],
                    axis=1,
                )
            )
            lanes = pl.ds(pl.multiple_of(group * 256 + side * 128, 128), 128)
            down.append(r.down_here[:, lanes])
        r.result[rows, :] += dot(block, jnp.concatenate(matrix, axis=0))
        r.low[rows, :] += dot_nt(block, jnp.concatenate(down, axis=1))

    w0, w1, w2 = weights
    k0, k1 = keys
    m0, m1 = mixes
    to_planes(w0)
    for ring in weights:
        ring.push_own(0)
        ring.hand(0, 0)
    normalize(1)
    w0.from_left(0)
    w0.from_right(0)
    to_planes(w1)
    w0.own(1)
    normalize(2)
    w0.own(2)
    w1.from_left(0)
    w1.from_right(0)
    w0.own(3)
    to_planes(w2)
    normalize(3)
    w0.from_left(1)
    w0.from_right(1)
    w0.from_left(2)
    w0.from_right(2)
    for copy in loads[10:]:
        copy.wait()
    reduced()
    w0.from_left(3)
    w0.from_right(3)
    w2.from_left(0)
    w2.from_right(0)
    for d in range(1, 4):
        w1.own(d)

    @pl.when(jnp.logical_not(stays))
    def _():
        turn_copy().start()

    @pl.when(stays)
    def _():
        copy = pltpu.make_async_copy(
            r.wo, r.columns.at[(turn_seq % 2) * 16 + (turn_seq // 2) % 4], r.load.at[22]
        )
        copy.start()
        copy.wait()

    for d in range(4):
        w0.across(d)
        accumulate(0, d)
    project_keys(0)
    for d in range(1, 4):
        w1.from_left(d)
        w1.from_right(d)
    for d in range(1, 4):
        w2.own(d)
    k0.from_left(0)
    k0.from_right(1)
    for d in range(4):
        w1.across(d)
        accumulate(1, d)
    k0.from_left(1)
    k0.from_right(0)
    k0.own(2)
    k0.own(3)
    for d in range(1, 4):
        w2.from_left(d)
        w2.from_right(d)
    pass_on(0, 0)
    pass_on(0, 1)
    project_keys(1)

    @pl.when(jnp.logical_not(stays))
    def _():
        columns.arrived(0, 0)

    columns.hand(0, 0)
    to_planes(columns)
    for d in range(4):
        w2.across(d)
        accumulate(2, d)
    project_queries(0)
    project_queries(1)

    diagonal(0)
    near(0)
    own_plane(0, 3)
    own_plane(0, 1)
    own_plane(0, 2)
    plane_before(0, 0)
    k1.from_left(0)
    k1.from_right(1)
    for d in range(2, 4):
        k0.from_left(d, False)
        k0.from_right(d, False)
    plane_before(0, 3)
    plane_before(0, 1)
    k1.from_left(1)
    k1.from_right(0)
    k1.own(2)
    k1.own(3)
    k0.across(2)
    k0.across(3)
    pass_on(1, 0)
    pass_on(1, 1)
    columns.push_own(0)
    for d in range(1, 4):
        columns.own(d)
    plane_before(0, 2)
    close(0)

    diagonal(1)
    near(1)
    own_plane(1, 3)
    own_plane(1, 1)
    own_plane(1, 2)
    plane_before(1, 0)
    for d in range(2, 4):
        k1.from_left(d, False)
        k1.from_right(d, False)
    plane_before(1, 3)
    plane_before(1, 1)
    for d in range(2, 4):
        m0.arrived(d, 0)
        push_mixed(0, d)
    k1.across(2)
    k1.across(3)
    plane_before(1, 2)
    close(1)

    for d in range(4):
        columns.from_left(d)
        columns.from_right(d)
    r.result[...] = jnp.zeros_like(r.result)
    r.low[...] = jnp.zeros_like(r.low)
    for d in range(2, 4):
        m1.arrived(d, 0)
        push_mixed(1, d)
    for d in range(4):
        columns.across(d)
    for d in range(4):
        for step in range(4):
            columns.handed(d, step)
    for d in range(4):
        for step in range(1, 4):
            m0.arrived(d, step)
        add(0, d)
    for d in range(4):
        for step in range(1, 4):
            m1.arrived(d, step)
        add(1, d)
    r.out[...] = (
        r.result[...] + ADAPTER_SCALING * dot(r.low[...].astype(BF16), r.up_here[...])
    ).astype(BF16)
    for ring in weights + keys + mixes + [columns]:
        ring.finish()

    @pl.when(jnp.logical_not(stays))
    def _():
        turn_copy().wait_send()


def rope_tables():
    frequency = ROPE_BASE ** (-2.0 * np.arange(64, dtype=np.float64) / HD)
    sign = np.concatenate([-np.ones(64), np.ones(64)])

    def table(positions):
        angles = positions[:, None] * np.concatenate([frequency, frequency])[None, :]
        return np.cos(angles), np.sin(angles) * sign

    tables = np.stack(table(np.arange(TOK, dtype=np.float64)))
    bases = np.stack(table(np.arange(32, dtype=np.float64) * TOK), axis=1)
    return tables.astype(np.float32), bases.astype(np.float32)


VMEM = pl.BlockSpec(memory_space=pltpu.VMEM)
ANY = pl.BlockSpec(memory_space=pl.ANY)
SMEM = pl.BlockSpec(memory_space=pltpu.SMEM)


def pass_through(out, sums, out_copy, sums_copy):
    out_copy[...] = out[...]
    sums_copy[...] = sums[...]


def body(
    activations,
    norm_gain,
    shifted,
    query_weight,
    key_weight,
    value_weight,
    output_weight,
    query_down,
    query_up,
    key_down,
    key_up,
    value_down,
    value_up,
    output_down,
    output_up_matrix,
):
    tables, bases = rope_tables()
    arguments = dict(
        act=(activations, ANY),
        gain=(norm_gain.reshape(1, D), VMEM),
        shifted=(shifted, SMEM),
        wq=(query_weight, ANY),
        wk=(key_weight, ANY),
        wv=(value_weight, ANY),
        wo=(output_weight, ANY),
        down_q=(query_down.T, ANY),
        up_q=(query_up, ANY),
        down_k=(key_down.T, ANY),
        up_k=(key_up, ANY),
        down_v=(value_down.T, ANY),
        up_v=(value_up, ANY),
        down_o=(output_down.T, ANY),
        up_o=(output_up_matrix, ANY),
        tables=(jnp.asarray(tables), ANY),
        bases=(jnp.asarray(bases), VMEM),
    )
    out, sums = pl.pallas_call(
        kernel,
        out_shape=(
            jax.ShapeDtypeStruct((TOK, 512), BF16),
            jax.ShapeDtypeStruct((2, TOK), F32),
        ),
        in_specs=[arguments[name][1] for name in INPUTS],
        out_specs=(VMEM, VMEM),
        scratch_shapes=list(SCRATCH.values()),
        compiler_params=pltpu.CompilerParams(
            collective_id=1, has_side_effects=True, vmem_limit_bytes=VMEM_BYTES
        ),
    )(*[arguments[name][0] for name in INPUTS])
    out, sums = pl.pallas_call(
        pass_through,
        out_shape=(
            jax.ShapeDtypeStruct((TOK, 512), BF16),
            jax.ShapeDtypeStruct((2, TOK), F32),
        ),
        in_specs=[VMEM, VMEM],
        out_specs=(VMEM, VMEM),
    )(out, sums)
    return out, sums.T


def solution(mesh):
    placed = (
        P("seq", None),
        P(),
        P(),
        P("seq", "head"),
        P("seq", "head"),
        P("seq", "head"),
        P("head", "seq"),
        P(),
        P(),
        P(),
        P(),
        P(),
        P(),
        P(),
        P(),
    )
    return jax.shard_map(
        body,
        mesh=mesh,
        in_specs=placed,
        out_specs=(P("seq", "head"), P("seq", "head")),
        check_vma=False,
    )
```
